32 devices in a mesh: fsdp: 16 (over z, y, core), tp: 2 (over x).
Axes of the slice: x: 2, y: 2, z: 4, core: 2. Of those that a mesh axis runs over, the one named last changes fastest.
Arguments:
- images: bfloat16 [16, 256, 6144], P('fsdp', None, 'tp'), may hold values from -6 to 6
- keep_index: int32 [16, 64], P('fsdp'), may hold values from 0 to 255, as said below
- teacher_weight: float32 [6144, 3072], P('fsdp', 'tp'), may hold values from -0.078125 to 0.078125
- student_weight: float32 [6144, 3072], P('fsdp', 'tp'), may hold values from -0.078125 to 0.078125
Outputs:
- teacher_next: float32 [6144, 3072], P('fsdp', 'tp')
- student_grad: float32 [6144, 3072], P('fsdp', 'tp')
The draws below stay inside these ranges and needn't reach their ends.
Inputs may be any that keep to these rules, and one draw needn't show every extreme that they name: `keep_index`: each image's 64 indices are distinct and increasing.
All inputs are finite; a program needn't handle non-finite values.
Results may differ from the reference program's by a relative error of at most 0.0048.
Values may be sent and summed in bfloat16 or wider, within the bound.
A program may use at most 128 MiB of HBM per device.

```python
import math
import jax
import jax.numpy as jnp
from jax import lax

D = 6144
PATCHES = 256
KEEP = 64
IMAGES = 16
PROJ = 3072


def draw_keep_index(key, part):
    streams = jax.random.split(jax.random.fold_in(key, 7), IMAGES)

    def one_image(stream):
        order = jax.random.permutation(stream, PATCHES)
        return jnp.sort(order[:KEEP]).astype(jnp.int32)
    return jax.vmap(one_image)(streams)


def steps_of(own_key, dims, shards, smallest, largest):
    gain = 1.0
    for position, shards_of in shards:
        heights = jax.random.uniform(jax.random.fold_in(jax.random.fold_in(own_key, 6), position), (shards_of,), jnp.float32, smallest / len(shards), largest / len(shards))
        gain = gain * jnp.repeat(jnp.exp(heights), dims[position] // shards_of).reshape((-1,) + (1,) * (len(dims) - 1 - position))
    return gain


def scatter_about(own_key, extent, scale, most, shards=(), dtype=jnp.bfloat16):
    result = jax.random.normal(own_key, extent, jnp.float32) * scale
    if len(shards) > 0:
        result = steps_of(own_key, extent, shards, -0.22, 0.18) * result
    return jnp.clip(result, min=-most, max=most).astype(dtype)


def setup_inputs(seed: int = 0) -> dict:
    key_list = jax.random.split(jax.random.key(seed), 5)
    return {
        "images": scatter_about(key_list[0], (IMAGES, PATCHES, D), 1.0, 6.0, ((0, 16), (2, 2))),
        "keep_index": draw_keep_index(jax.random.fold_in(key_list[4], 71), 0),
        "teacher_weight": scatter_about(key_list[2], (D, PROJ), D ** -0.5, 0.078125, ((0, 16), (1, 2)), jnp.float32),
        "student_weight": scatter_about(key_list[3], (D, PROJ), D ** -0.5, 0.078125, ((0, 16), (1, 2)), jnp.float32),
    }


def layer_norm(values):
    floats = values.astype(jnp.float32)
    centre = lax.optimization_barrier(jnp.mean(floats, axis=-1, keepdims=True))
    centred = floats - centre
    spread = lax.optimization_barrier(jnp.mean(centred * centred, axis=-1, keepdims=True))
    return (centred * lax.rsqrt(spread + 1e-06)).astype(jnp.bfloat16)

def pick_rows(table, index):
    return jax.vmap(lambda block, rows: block[rows])(table, index)

def reference(images, keep_index, teacher_weight, student_weight):
    teacher_next = 0.999 * teacher_weight + (1.0 - 0.999) * student_weight
    teacher_panel = teacher_next.astype(jnp.bfloat16)
    student_panel = student_weight.astype(jnp.bfloat16)
    normed = layer_norm(images)
    teacher_out = jnp.dot(normed.reshape(-1, D), teacher_panel, preferred_element_type=jnp.float32)
    teacher_out = teacher_out.reshape(IMAGES, PATCHES, -1)
    centre = lax.optimization_barrier(jnp.mean(teacher_out, axis=1, keepdims=True))
    centred = teacher_out - centre
    spread = lax.optimization_barrier(jnp.mean(centred * centred, axis=1, keepdims=True))
    target = centred * lax.rsqrt(spread + 1e-05)
    picked = pick_rows(normed, keep_index).reshape(-1, D)
    target_kept = pick_rows(target, keep_index).reshape(picked.shape[0], -1)
    student_out = jnp.dot(picked, student_panel, preferred_element_type=jnp.float32)
    error = ((student_out - target_kept) * (1.0 / math.sqrt(IMAGES * KEEP))).astype(jnp.bfloat16)
    student_grad = jnp.dot(picked.T, error, preferred_element_type=jnp.float32)
    return (teacher_next, student_grad)
```

```python
import math

import jax
import jax.numpy as jnp
from jax import lax
from jax.sharding import PartitionSpec as P

D = 6144


def layer_norm(values):
    floats = values.astype(jnp.float32)
    centre = jnp.mean(floats, axis=-1, keepdims=True)
    centred = floats - centre
    spread = jnp.mean(centred * centred, axis=-1, keepdims=True)
    return (centred * lax.rsqrt(spread + 1e-06)).astype(jnp.bfloat16)


def pick_rows(table, index):
    return jax.vmap(lambda block, rows: block[rows])(table, index)


def row_product(features, piece):
    return jnp.dot(features, piece, preferred_element_type=jnp.float32)


def whole_features(images):
    if lax.axis_size("tp") != 2:
        return lax.all_gather(images, "tp", axis=2, tiled=True)
    other = lax.ppermute(images, "tp", [(0, 1), (1, 0)])
    first = lax.axis_index("tp") == 0
    return jnp.concatenate(
        [jnp.where(first, images, other), jnp.where(first, other, images)], axis=2
    )


def shards(images, keep_index, teacher_weight, student_weight):
    img_count = images.shape[0]
    patch_count = images.shape[1]
    keep_count = keep_index.shape[1]
    columns_dev = teacher_weight.shape[1]
    teacher_next = 0.999 * teacher_weight + (1.0 - 0.999) * student_weight
    teacher_panel = teacher_next.astype(jnp.bfloat16)
    student_panel = student_weight.astype(jnp.bfloat16)
    whole_panel = lax.all_gather(teacher_panel, "fsdp", axis=0, tiled=True)
    normed = layer_norm(whole_features(images))
    flat_all = normed.reshape(img_count * patch_count, D)
    picked = pick_rows(normed, keep_index).reshape(img_count * keep_count, D)
    owned = lax.all_to_all(picked, "fsdp", split_axis=1, concat_axis=0, tiled=True)
    partial = row_product(owned, student_panel).astype(jnp.bfloat16)
    student_out = lax.psum_scatter(partial, "fsdp", scatter_dimension=0, tiled=True)
    student_out = student_out.astype(jnp.float32)
    teacher_out = row_product(flat_all, whole_panel)
    teacher_out = teacher_out.reshape(img_count, patch_count, columns_dev)
    centre = jnp.mean(teacher_out, axis=1, keepdims=True)
    centred_out = teacher_out - centre
    spread = jnp.mean(centred_out * centred_out, axis=1, keepdims=True)
    target = centred_out * lax.rsqrt(spread + 1e-05)
    target_kept = pick_rows(target, keep_index).reshape(img_count * keep_count, columns_dev)
    total_kept = img_count * keep_count * lax.axis_size("fsdp")
    error = ((student_out - target_kept) * (1.0 / math.sqrt(total_kept))).astype(jnp.bfloat16)
    student_grad = lax.dot_general(
        owned,
        lax.all_gather(error, "fsdp", axis=0, tiled=True),
        (((0,), (0,)), ((), ())),
        preferred_element_type=jnp.float32,
    )
    return (teacher_next, student_grad)


def solution(mesh):
    placed = (P("fsdp", None, "tp"), P("fsdp", None), P("fsdp", "tp"), P("fsdp", "tp"))
    return jax.shard_map(
        shards,
        mesh=mesh,
        in_specs=placed,
        out_specs=(P("fsdp", "tp"), P("fsdp", "tp")),
        check_vma=False,
    )
```

```python
import functools
import math

import jax
import jax.numpy as jnp
from jax import lax
from jax.experimental import pallas as pl
from jax.experimental.pallas import tpu as pltpu
from jax.sharding import PartitionSpec as P

D = 6144


def layer_norm(values):
    floats = values.astype(jnp.float32)
    centre = jnp.mean(floats, axis=-1, keepdims=True)
    centred = floats - centre
    spread = jnp.mean(centred * centred, axis=-1, keepdims=True)
    return (centred * lax.rsqrt(spread + 1e-06)).astype(jnp.bfloat16)


def pick_rows(table, index):
    return jax.vmap(lambda block, rows: block[rows])(table, index)


def row_product(features, piece):
    return jnp.dot(features, piece, preferred_element_type=jnp.float32)


def whole_features(images):
    if lax.axis_size("tp") != 2:
        return lax.all_gather(images, "tp", axis=2, tiled=True)
    other = lax.ppermute(images, "tp", [(0, 1), (1, 0)])
    first = lax.axis_index("tp") == 0
    return jnp.concatenate(
        [jnp.where(first, images, other), jnp.where(first, other, images)], axis=2
    )


def shards(images, keep_index, teacher_weight, student_weight):
    img_count = images.shape[0]
    patch_count = images.shape[1]
    keep_count = keep_index.shape[1]
    columns_dev = teacher_weight.shape[1]
    teacher_next = 0.999 * teacher_weight + (1.0 - 0.999) * student_weight
    teacher_panel = teacher_next.astype(jnp.bfloat16)
    student_panel = student_weight.astype(jnp.bfloat16)
    whole_panel = lax.all_gather(teacher_panel, "fsdp", axis=0, tiled=True)
    normed = layer_norm(whole_features(images))
    flat_all = normed.reshape(img_count * patch_count, D)
    picked = pick_rows(normed, keep_index).reshape(img_count * keep_count, D)
    owned = lax.all_to_all(picked, "fsdp", split_axis=1, concat_axis=0, tiled=True)
    partial = row_product(owned, student_panel).astype(jnp.bfloat16)
    student_out = lax.psum_scatter(partial, "fsdp", scatter_dimension=0, tiled=True)
    student_out = student_out.astype(jnp.float32)
    teacher_out = row_product(flat_all, whole_panel)
    teacher_out = teacher_out.reshape(img_count, patch_count, columns_dev)
    centre = jnp.mean(teacher_out, axis=1, keepdims=True)
    centred_out = teacher_out - centre
    spread = jnp.mean(centred_out * centred_out, axis=1, keepdims=True)
    target = centred_out * lax.rsqrt(spread + 1e-05)
    target_kept = pick_rows(target, keep_index).reshape(img_count * keep_count, columns_dev)
    total_kept = img_count * keep_count * lax.axis_size("fsdp")
    error = ((student_out - target_kept) * (1.0 / math.sqrt(total_kept))).astype(jnp.bfloat16)
    student_grad = lax.dot_general(
        owned,
        lax.all_gather(error, "fsdp", axis=0, tiled=True),
        (((0,), (0,)), ((), ())),
        preferred_element_type=jnp.float32,
    )
    return (teacher_next, student_grad)


MESH = pl.DeviceIdType.MESH
LANE_BLOCK = 384


def fused(n, total_kept, pick, images, tw, sw, tnext, grad, xbuf, nbuf, sbuf, wt, ws, acc, tsib,
          pbuf, owned, pf, h1s, h1r, h2s, h2r, h3s, h3r, ebuf, loc, xs, xr, rs, rr, ns, nr,
          as_, ar, h1ss, h1rs, h2ss, h2rs, h3ss, h3rs, ts, tr, es, er, bs, br):
    f = lax.axis_index("fsdp")
    t = lax.axis_index("tp")
    chips = n // 2
    zs = chips // 2
    core = lax.rem(f, 2)
    other = 1 - core
    chip = lax.div(f, 2)
    y = lax.rem(chip, 2)
    z = lax.div(chip, 2)
    place = (1 - y) * z + y * (chips - 1 - z)
    patches = images.shape[0]
    depth = tw.shape[0]
    blocks = tw.shape[1] // LANE_BLOCK
    half = blocks // 2
    keep = pick.shape[0]

    def chip_at(position):
        position = lax.rem(position + 2 * chips, chips)
        back = lax.div(position, zs)
        return (1 - back) * 2 * position + back * (2 * (chips - 1 - position) + 1)

    sibling = (2 * chip + other, t)
    ahead = (2 * chip_at(place + 1) + core, t)
    behind = (2 * chip_at(place - 1) + core, t)
    route = (ahead, behind)

    def remote(src, dst, send, recv, device):
        return pltpu.make_async_remote_copy(
            src_ref=src, dst_ref=dst, send_sem=send, recv_sem=recv,
            device_id=device, device_id_type=MESH)

    barrier = pltpu.get_barrier_semaphore()
    for j in range(1, n):
        pl.semaphore_signal(barrier, inc=1, device_id=(lax.rem(f + j, n), t), device_id_type=MESH)
    pl.semaphore_signal(barrier, inc=1, device_id=(f, 1 - t), device_id_type=MESH)
    pl.semaphore_wait(barrier, n)

    x_out = remote(images, xbuf.at[t], xs.at[0], xr.at[0], (f, 1 - t))
    x_out.start()
    x_own = pltpu.make_async_copy(images, xbuf.at[t], loc.at[0])
    x_own.start()

    tile = 32

    @pl.loop(0, depth // tile)
    def _(i):
        rows = pl.ds(pl.multiple_of(i * tile, tile), tile)
        student = sw[rows, :]
        following = 0.999 * tw[rows, :] + (1.0 - 0.999) * student
        tnext[rows, :] = following
        for q in range(blocks):
            columns = slice(q * LANE_BLOCK, (q + 1) * LANE_BLOCK)
            wt[q, chip, rows, :] = following[:, columns].astype(jnp.bfloat16)
            ws[q, rows, :] = student[:, columns].astype(jnp.bfloat16)

    def ring_copy(q, s, source):
        ref = wt.at[q, source]
        return remote(ref, ref, rs.at[q, s], rr.at[q, s], route[q // half])

    def source_of(q, s):
        return chip_at(place - s) if q < half else chip_at(place + s)

    for q in range(blocks):
        ring_copy(q, 0, chip).start()

    def pump(s):
        for q in range(blocks):
            arrived = source_of(q, s + 1)
            ring_copy(q, s, arrived).wait_recv()
            if s < chips - 2:
                ring_copy(q, s + 1, arrived).start()

    acc[...] = jnp.zeros_like(acc)

    def consume(low, high):
        @pl.loop(low, high)
        def _(s):
            @pl.loop(0, blocks)
            def _(q):
                way = lax.div(q, half)
                source = chip_at(place - s + 2 * way * s)
                panel = wt[q, source]
                acc[0, q] += jnp.dot(nbuf[core, source], panel, preferred_element_type=jnp.float32)
                acc[1, q] += jnp.dot(sbuf[source], panel, preferred_element_type=jnp.float32)

    pump(0)
    pump(1)
    pump(2)

    x_own.wait()
    remote(images, xbuf.at[1 - t], xs.at[0], xr.at[0], (f, 1 - t)).wait_recv()
    features = n * depth
    per_side = n // 2

    @pl.loop(0, patches // 16)
    def _(i):
        rows = pl.ds(pl.multiple_of(i * 16, 16), 16)
        sides = [xbuf[g, rows, :].astype(jnp.float32) for g in range(2)]
        centre = sum(jnp.sum(v, axis=1, keepdims=True) for v in sides) * (1.0 / features)
        sides = [v - centre for v in sides]
        spread = sum(jnp.sum(v * v, axis=1, keepdims=True) for v in sides) * (1.0 / features)
        scale = lax.rsqrt(spread + 1e-06)
        for g in range(2):
            scaled = (sides[g] * scale).astype(jnp.bfloat16)
            for j in range(per_side):
                owner = g * per_side + j
                nbuf[owner % 2, owner // 2, rows, :] = scaled[:, j * depth:(j + 1) * depth]

    n_out = remote(nbuf.at[other], sbuf, ns.at[0], nr.at[0], sibling)
    n_out.start()

    @pl.loop(0, chips)
    def _(c):
        for k in range(2):
            pbuf[k, c] = jnp.dot(
                pick[...], nbuf[k, c], preferred_element_type=jnp.float32).astype(jnp.bfloat16)

    def swap_copy(j, to):
        return remote(pbuf.at[lax.rem(to, 2), lax.div(to, 2)], owned.at[core, chip],
                      as_.at[j - 1], ar.at[j - 1], (to, t))

    for j in range(1, n):
        swap_copy(j, lax.rem(f + j, n)).start()
    owned[core, chip] = pbuf[core, chip]

    pump(3)
    n_out.wait_recv()
    consume(0, 4)

    for j in range(1, n):
        origin = lax.rem(f + n - j, n)
        remote(pbuf.at[0, 0], owned.at[lax.rem(origin, 2), lax.div(origin, 2)],
               as_.at[j - 1], ar.at[j - 1], (origin, t)).wait_recv()

    rows_core = chips * keep

    @pl.loop(0, blocks)
    def _(q):
        panel = ws[q]
        send = jnp.dot(owned[other].reshape(rows_core, depth), panel,
                       preferred_element_type=jnp.float32)
        h1s[q] = send.astype(jnp.bfloat16).reshape(zs, 2, keep, LANE_BLOCK)
        mine = jnp.dot(owned[core].reshape(rows_core, depth), panel,
                       preferred_element_type=jnp.float32)
        pf[q] = mine.reshape(zs, 2, keep, LANE_BLOCK)

    h1 = remote(h1s, h1r, h1ss.at[0], h1rs.at[0], sibling)
    h1.start()
    pump(4)
    h1.wait_recv()

    @pl.loop(0, blocks)
    def _(q):
        @pl.loop(0, zs)
        def _(g):
            h2s[q, g] = (pf[q, g, 1 - y] + h1r[q, g, 1 - y].astype(jnp.float32)).astype(jnp.bfloat16)
            pf[q, g, y] += h1r[q, g, y].astype(jnp.float32)

    across = (2 * (2 * z + 1 - y) + core, t)
    h2 = remote(h2s, h2r, h2ss.at[0], h2rs.at[0], across)
    h2.start()
    consume(4, 6)
    pump(5)
    h2.wait_recv()

    @pl.loop(0, zs)
    def _(g):
        @pl.loop(0, blocks)
        def _(q):
            value = pf[q, g, y] + h2r[q, g].astype(jnp.float32)
            pf[q, g, y] = value
            h3s[g, q] = value.astype(jnp.bfloat16)

    def level_copy(j):
        to = lax.rem(z + j, zs)
        return remote(h3s.at[to], h3r.at[j - 1], h3ss.at[j - 1], h3rs.at[j - 1],
                      (2 * (2 * to + y) + core, t))

    for j in range(1, zs):
        level_copy(j).start()
    consume(6, 7)
    pump(6)
    consume(7, 8)

    def half_copy(q):
        return remote(acc.at[1, q], tsib.at[q], ts.at[q], tr.at[q], sibling)

    for q in range(blocks):
        half_copy(q).start()
    for j in range(1, zs):
        level_copy(j).wait_recv()

    for q in range(blocks):
        half_copy(q).wait_recv()
        value = acc[0, q] + tsib[q]
        centre = jnp.sum(value, axis=0, keepdims=True) * (1.0 / patches)
        value = value - centre
        spread = jnp.sum(value * value, axis=0, keepdims=True) * (1.0 / patches)
        target = value * lax.rsqrt(spread + 1e-05)
        upper = target.astype(jnp.bfloat16)
        lower = (target - upper.astype(jnp.float32)).astype(jnp.bfloat16)
        kept = (jnp.dot(pick[...], upper, preferred_element_type=jnp.float32)
                + jnp.dot(pick[...], lower, preferred_element_type=jnp.float32))
        student = pf[q, z, y]
        for j in range(1, zs):
            student = student + h3r[j - 1, q].astype(jnp.float32)
        ebuf[core, chip, q] = ((student - kept) * (1.0 / math.sqrt(total_kept))).astype(jnp.bfloat16)

    def error_copy(way, s, source):
        ref = ebuf.at[core, source, pl.ds(way * half, half)]
        return remote(ref, ref, es.at[way, s], er.at[way, s], route[way])

    def beside_copy(way, s, source, owner):
        ref = ebuf.at[owner, source, pl.ds(way * half, half)]
        return remote(ref, ref, bs.at[way, s], br.at[way, s], sibling)

    def turn(way, s):
        return chip_at(place - s) if way == 0 else chip_at(place + s)

    for way in range(2):
        error_copy(way, 0, chip).start()
    for way in range(2):
        beside_copy(way, 0, chip, core).start()
    for s in range(chips - 1):
        for way in range(2):
            arrived = turn(way, s + 1)
            error_copy(way, s, arrived).wait_recv()
            if s < chips - 2:
                error_copy(way, s + 1, arrived).start()
            beside_copy(way, s + 1, arrived, core).start()
    for s in range(chips):
        for way in range(2):
            beside_copy(way, s, turn(way, s), other).wait_recv()

    features_rows = owned[...].reshape(n * keep, depth)
    for q in range(blocks):
        errors = ebuf[:, :, q].reshape(n * keep, LANE_BLOCK)
        grad[:, q * LANE_BLOCK:(q + 1) * LANE_BLOCK] = lax.dot_general(
            features_rows, errors, (((0,), (0,)), ((), ())), preferred_element_type=jnp.float32)

    x_out.wait_send()
    n_out.wait_send()
    h1.wait_send()
    h2.wait_send()
    for s in range(chips - 1):
        for q in range(blocks):
            ring_copy(q, s, chip).wait_send()
        for way in range(2):
            error_copy(way, s, chip).wait_send()
    for s in range(chips):
        for way in range(2):
            beside_copy(way, s, chip, core).wait_send()
    for j in range(1, n):
        swap_copy(j, lax.rem(f + j, n)).wait_send()
    for j in range(1, zs):
        level_copy(j).wait_send()
    for q in range(blocks):
        half_copy(q).wait_send()


def fused_shards(images, keep_index, teacher_weight, student_weight):
    n = lax.axis_size("fsdp")
    patches, width = images.shape[1:]
    keep = keep_index.shape[1]
    depth, columns = teacher_weight.shape
    chips, zs, blocks = n // 2, n // 4, columns // LANE_BLOCK
    pick = (keep_index[0][:, None] == jnp.arange(patches)[None, :]).astype(jnp.bfloat16)
    bf, fl = jnp.bfloat16, jnp.float32
    dma = pltpu.SemaphoreType.DMA
    vm = pltpu.VMEM
    scratch = [
        vm((2, patches, width), bf),
        vm((2, chips, patches, depth), bf),
        vm((chips, patches, depth), bf),
        vm((blocks, chips, depth, LANE_BLOCK), bf),
        vm((blocks, depth, LANE_BLOCK), bf),
        vm((2, blocks, patches, LANE_BLOCK), fl),
        vm((blocks, patches, LANE_BLOCK), fl),
        vm((2, chips, keep, depth), bf),
        vm((2, chips, keep, depth), bf),
        vm((blocks, zs, 2, keep, LANE_BLOCK), fl),
        vm((blocks, zs, 2, keep, LANE_BLOCK), bf),
        vm((blocks, zs, 2, keep, LANE_BLOCK), bf),
        vm((blocks, zs, keep, LANE_BLOCK), bf),
        vm((blocks, zs, keep, LANE_BLOCK), bf),
        vm((zs, blocks, keep, LANE_BLOCK), bf),
        vm((zs - 1, blocks, keep, LANE_BLOCK), bf),
        vm((2, chips, blocks, keep, LANE_BLOCK), bf),
        dma((1,)), dma((1,)), dma((1,)),
        dma((blocks, chips - 1)), dma((blocks, chips - 1)),
        dma((1,)), dma((1,)),
        dma((n - 1,)), dma((n - 1,)),
        dma((1,)), dma((1,)), dma((1,)), dma((1,)),
        dma((zs - 1,)), dma((zs - 1,)),
        dma((blocks,)), dma((blocks,)),
        dma((2, chips - 1)), dma((2, chips - 1)),
        dma((2, chips)), dma((2, chips)),
    ]
    out = jax.ShapeDtypeStruct((depth, columns), fl)
    return pl.pallas_call(
        functools.partial(fused, n, keep * n),
        out_shape=(out, out),
        in_specs=[pl.BlockSpec(memory_space=pltpu.VMEM)] * 4,
        out_specs=(pl.BlockSpec(memory_space=pltpu.VMEM),) * 2,
        scratch_shapes=scratch,
        compiler_params=pltpu.CompilerParams(
            collective_id=0, has_side_effects=True, vmem_limit_bytes=60 * 2**20),
        cost_estimate=pl.CostEstimate(
            flops=2 * n * depth * columns * (patches + 2 * keep), bytes_accessed=2**24, transcendentals=0),
    )(pick, images[0], teacher_weight, student_weight)


def solution(mesh):
    placed = (P("fsdp", None, "tp"), P("fsdp", None), P("fsdp", "tp"), P("fsdp", "tp"))
    fits = mesh.shape["tp"] == 2 and mesh.shape["fsdp"] == 16
    return jax.shard_map(
        fused_shards if fits else shards,
        mesh=mesh,
        in_specs=placed,
        out_specs=(P("fsdp", "tp"), P("fsdp", "tp")),
        check_vma=False,
    )
```

```python
import functools
import math

import jax
import jax.numpy as jnp
from jax import lax
from jax.experimental import pallas as pl
from jax.experimental.pallas import tpu as pltpu
from jax.sharding import PartitionSpec as P

D = 6144


def layer_norm(values):
    floats = values.astype(jnp.float32)
    centre = jnp.mean(floats, axis=-1, keepdims=True)
    centred = floats - centre
    spread = jnp.mean(centred * centred, axis=-1, keepdims=True)
    return (centred * lax.rsqrt(spread + 1e-06)).astype(jnp.bfloat16)


def pick_rows(table, index):
    return jax.vmap(lambda block, rows: block[rows])(table, index)


def row_product(features, piece):
    return jnp.dot(features, piece, preferred_element_type=jnp.float32)


def whole_features(images):
    if lax.axis_size("tp") != 2:
        return lax.all_gather(images, "tp", axis=2, tiled=True)
    other = lax.ppermute(images, "tp", [(0, 1), (1, 0)])
    first = lax.axis_index("tp") == 0
    return jnp.concatenate(
        [jnp.where(first, images, other), jnp.where(first, other, images)], axis=2
    )


def shards(images, keep_index, teacher_weight, student_weight):
    img_count = images.shape[0]
    patch_count = images.shape[1]
    keep_count = keep_index.shape[1]
    columns_dev = teacher_weight.shape[1]
    teacher_next = 0.999 * teacher_weight + (1.0 - 0.999) * student_weight
    teacher_panel = teacher_next.astype(jnp.bfloat16)
    student_panel = student_weight.astype(jnp.bfloat16)
    whole_panel = lax.all_gather(teacher_panel, "fsdp", axis=0, tiled=True)
    normed = layer_norm(whole_features(images))
    flat_all = normed.reshape(img_count * patch_count, D)
    picked = pick_rows(normed, keep_index).reshape(img_count * keep_count, D)
    owned = lax.all_to_all(picked, "fsdp", split_axis=1, concat_axis=0, tiled=True)
    partial = row_product(owned, student_panel).astype(jnp.bfloat16)
    student_out = lax.psum_scatter(partial, "fsdp", scatter_dimension=0, tiled=True)
    student_out = student_out.astype(jnp.float32)
    teacher_out = row_product(flat_all, whole_panel)
    teacher_out = teacher_out.reshape(img_count, patch_count, columns_dev)
    centre = jnp.mean(teacher_out, axis=1, keepdims=True)
    centred_out = teacher_out - centre
    spread = jnp.mean(centred_out * centred_out, axis=1, keepdims=True)
    target = centred_out * lax.rsqrt(spread + 1e-05)
    target_kept = pick_rows(target, keep_index).reshape(img_count * keep_count, columns_dev)
    total_kept = img_count * keep_count * lax.axis_size("fsdp")
    error = ((student_out - target_kept) * (1.0 / math.sqrt(total_kept))).astype(jnp.bfloat16)
    student_grad = lax.dot_general(
        owned,
        lax.all_gather(error, "fsdp", axis=0, tiled=True),
        (((0,), (0,)), ((), ())),
        preferred_element_type=jnp.float32,
    )
    return (teacher_next, student_grad)


MESH = pl.DeviceIdType.MESH
LANE_BLOCK = 384


def fused(n, total_kept, pick, images, tw, sw, tnext, grad, stat, stat_in, nbuf, xk, wt, ws,
          pt, os_, or_, ys_, yr_, pb, pxs, owned, turned, pf, h1s, h1r, h2s, h2r, h3s, h3r, ebuf,
          sts, str_, xs, xr, ls, lr, ps, pr, as_, ar, ss, sr, h1ss, h1rs, h2ss, h2rs, h3ss, h3rs,
          oss, ors, yss, yrs, zss, zrs, ess, ers, bss, brs):
    f = lax.axis_index("fsdp")
    t = lax.axis_index("tp")
    zs = n // 4
    side = n // 2
    z = lax.div(f, 4)
    spot = lax.rem(f, 4)
    y = lax.div(spot, 2)
    core = lax.rem(spot, 2)
    other = 1 - core
    patches, width = images.shape
    depth = tw.shape[0]
    blocks = tw.shape[1] // LANE_BLOCK
    keep = pick.shape[0]
    part = keep // 2
    sibling = (4 * z + 2 * y + other, t)
    across = (4 * z + 2 * (1 - y) + core, t)
    mirror = (f, 1 - t)

    def remote(src, dst, send, recv, device):
        return pltpu.make_async_remote_copy(
            src_ref=src, dst_ref=dst, send_sem=send, recv_sem=recv,
            device_id=device, device_id_type=MESH)

    barrier = pltpu.get_barrier_semaphore()
    for j in range(1, n):
        pl.semaphore_signal(barrier, inc=1, device_id=(lax.rem(f + j, n), t), device_id_type=MESH)
    for j in range(4):
        pl.semaphore_signal(
            barrier, inc=1, device_id=(4 * z + lax.rem(spot + j, 4), 1 - t), device_id_type=MESH)
    pl.semaphore_wait(barrier, n + 3)

    lane = lax.broadcasted_iota(jnp.int32, (16, 128), 1)

    @pl.loop(0, patches // 16)
    def _(i):
        rows = pl.ds(pl.multiple_of(i * 16, 16), 16)
        values = images[rows, :].astype(jnp.float32)
        centre = jnp.sum(values, axis=1, keepdims=True) * (1.0 / width)
        values = values - centre
        spread = jnp.sum(values * values, axis=1, keepdims=True)
        stat[rows, :] = jnp.where(lane < 64, centre, spread)

    stats = remote(stat, stat_in, sts.at[0], str_.at[0], mirror)
    stats.start()

    tile = 32

    @pl.loop(0, depth // tile)
    def _(i):
        rows = pl.ds(pl.multiple_of(i * tile, tile), tile)
        student = sw[rows, :]
        following = 0.999 * tw[rows, :] + (1.0 - 0.999) * student
        tnext[rows, :] = following
        for q in range(blocks):
            columns = slice(q * LANE_BLOCK, (q + 1) * LANE_BLOCK)
            wt[q, z, rows, :] = following[:, columns].astype(jnp.bfloat16)
            ws[q, rows, :] = student[:, columns].astype(jnp.bfloat16)

    def line_copy(way, q, i, source, to):
        ref = wt.at[q, source]
        return remote(ref, ref, ls.at[way, q, i], lr.at[way, q, i], to)

    down = (f - 4, t)
    up = (f + 4, t)
    for q in range(blocks):
        @pl.when(z > 0)
        def _():
            line_copy(0, q, 0, z, down).start()

        @pl.when(z < zs - 1)
        def _():
            line_copy(1, q, 0, z, up).start()

    def pump(i, q):
        @pl.when(z + 1 + i < zs)
        def _():
            line_copy(0, q, i, z + 1 + i, sibling).wait_recv()
            if i < zs - 2:
                @pl.when(z > 0)
                def _():
                    line_copy(0, q, i + 1, z + 1 + i, down).start()

        @pl.when(z - 1 - i >= 0)
        def _():
            line_copy(1, q, i, z - 1 - i, sibling).wait_recv()
            if i < zs - 2:
                @pl.when(z < zs - 1)
                def _():
                    line_copy(1, q, i + 1, z - 1 - i, up).start()

    stats.wait_recv()

    @pl.loop(0, patches // 16)
    def _(i):
        rows = pl.ds(pl.multiple_of(i * 16, 16), 16)
        here, there = stat[rows, :], stat_in[rows, :]
        centre = (here[:, 0:1] + there[:, 0:1]) * 0.5
        apart = here[:, 0:1] - there[:, 0:1]
        spread = (here[:, 64:65] + there[:, 64:65]) * (0.5 / width) + apart * apart * 0.25
        scaled = ((images[rows, :].astype(jnp.float32) - centre) * lax.rsqrt(spread + 1e-06)).astype(jnp.bfloat16)
        for j in range(side):
            nbuf[j % 4 // 2, j % 2, j // 4, rows, :] = scaled[:, j * depth:(j + 1) * depth]

    @pl.loop(0, side // 4)
    def _(level):
        for j in range(4):
            rows = jnp.dot(pick[...], nbuf[j // 2, j % 2, level],
                           preferred_element_type=jnp.float32).astype(jnp.bfloat16)
            pb[side * t + 4 * level + j] = rows[:part]
            pxs[4 * level + j] = rows[part:]

    kept_out = remote(pxs, pb.at[pl.ds(side * t, side)], ps.at[0], pr.at[0], mirror)
    kept_out.start()

    def feature_copy(plane, j):
        to = lax.rem(spot + j, 4)
        return remote(nbuf.at[lax.div(to, 2), lax.rem(to, 2)], xk.at[y, core, pl.ds(2 * t, 2)],
                      xs.at[plane, j], xr.at[plane, j],
                      (4 * z + to, t if plane == 0 else 1 - t))

    xk[y, core, pl.ds(2 * t, 2)] = nbuf[y, core]
    kept_in = remote(pxs, pb.at[pl.ds(side * (1 - t), side)], ps.at[0], pr.at[0], mirror)
    kept_in.wait_recv()

    def half_of(device):
        return lax.rem(t + lax.div(device, side), 2)

    def swap_copy(j):
        to = lax.rem(f + j, n)
        return remote(pb.at[to], owned.at[half_of(to), core, y, z], as_.at[j - 1], ar.at[j - 1], (to, t))

    mine = half_of(f)
    for j in range(1, n):
        swap_copy(j).start()
    owned[mine, core, y, z] = pb[f]
    for j in range(1, 4):
        feature_copy(0, j).start()
    for j in range(4):
        feature_copy(1, j).start()

    for q in range(blocks):
        pump(0, q)

    for j in range(1, n):
        origin = lax.rem(f + n - j, n)
        remote(pb.at[0],
               owned.at[mine, lax.rem(origin, 2), lax.div(lax.rem(origin, 4), 2), lax.div(origin, 4)],
               as_.at[j - 1], ar.at[j - 1], (origin, t)).wait_recv()
    halves = remote(owned.at[mine], owned.at[mine], ss.at[0], sr.at[0], mirror)
    halves.start()
    remote(owned.at[1 - mine], owned.at[1 - mine], ss.at[0], sr.at[0], mirror).wait_recv()

    split = (2, 2, zs, part, LANE_BLOCK)
    rows_core = 4 * zs * part

    @pl.loop(0, blocks)
    def _(q):
        panel = ws[q]
        send = jnp.dot(owned[:, other].reshape(rows_core, depth), panel,
                       preferred_element_type=jnp.float32)
        h1s[q] = send.astype(jnp.bfloat16).reshape(split)
        own = jnp.dot(owned[:, core].reshape(rows_core, depth), panel,
                      preferred_element_type=jnp.float32)
        pf[q] = own.reshape(split)

    h1 = remote(h1s, h1r, h1ss.at[0], h1rs.at[0], sibling)
    h1.start()
    for g in range(2):
        turned[g] = owned[g].reshape(rows_core, depth).T
    h1.wait_recv()

    @pl.loop(0, blocks)
    def _(q):
        for g in range(2):
            h2s[q, g] = (pf[q, g, 1 - y] + h1r[q, g, 1 - y].astype(jnp.float32)).astype(jnp.bfloat16)
            pf[q, g, y] += h1r[q, g, y].astype(jnp.float32)

    h2 = remote(h2s, h2r, h2ss.at[0], h2rs.at[0], across)
    h2.start()

    for q in range(blocks):
        pump(1, q)
    h2.wait_recv()

    @pl.loop(0, zs)
    def _(level):
        @pl.loop(0, blocks)
        def _(q):
            for g in range(2):
                value = pf[q, g, y, level] + h2r[q, g, level].astype(jnp.float32)
                pf[q, g, y, level] = value
                h3s[level, q, g] = value.astype(jnp.bfloat16)

    def level_copy(j):
        to = lax.rem(z + j, zs)
        return remote(h3s.at[to], h3r.at[j - 1], h3ss.at[j - 1], h3rs.at[j - 1], (4 * to + spot, t))

    for j in range(1, zs):
        level_copy(j).start()

    def feature_wait(plane, j):
        origin = lax.rem(spot + 4 - j, 4)
        first = 2 * t if plane == 0 else 2 * (1 - t)
        remote(nbuf.at[0, 0], xk.at[lax.div(origin, 2), lax.rem(origin, 2), pl.ds(first, 2)],
               xs.at[plane, j], xr.at[plane, j], sibling).wait_recv()

    for j in range(1, 4):
        feature_wait(0, j)
    for j in range(4):
        feature_wait(1, j)

    def sibling_copy(q):
        return remote(os_.at[q], or_.at[q], oss.at[q], ors.at[q], sibling)

    def across_copy(q):
        return remote(ys_.at[q], yr_.at[q], yss.at[q], yrs.at[q], across)

    def error_level(q, j):
        ref = ebuf.at[q, core, y, z]
        return remote(ref, ref, zss.at[q, j - 1], zrs.at[q, j - 1], (4 * lax.rem(z + j, zs) + spot, t))

    def error_across(q, row):
        ref = ebuf.at[q, core, row]
        return remote(ref, ref, ess.at[q], ers.at[q], across)

    def error_sibling(q, owner):
        ref = ebuf.at[q, owner]
        return remote(ref, ref, bss.at[q], brs.at[q], sibling)

    def product(q):
        if zs > 2:
            pump(zs - 2, q)

        @pl.loop(0, 2)
        def _(row):
            for target, owner in ((os_, other), (pt, core)):
                total = jnp.dot(xk[row, owner, 0], wt[q, 0], preferred_element_type=jnp.float32)
                for level in range(1, zs):
                    total += jnp.dot(xk[row, owner, level], wt[q, level],
                                     preferred_element_type=jnp.float32)
                target[q, row] = total

        sibling_copy(q).start()

    def cores_add(q):
        sibling_copy(q).wait_recv()
        ys_[q] = (pt[q, 1 - y] + or_[q, 1 - y]).astype(jnp.bfloat16)
        across_copy(q).start()
        pt[q, y] += or_[q, y]

    def error_of(q):
        if q == 0:
            for j in range(1, zs):
                level_copy(j).wait_recv()
        across_copy(q).wait_recv()
        value = pt[q, y] + yr_[q].astype(jnp.float32)
        centre = jnp.sum(value, axis=0, keepdims=True) * (1.0 / patches)
        value = value - centre
        spread = jnp.sum(value * value, axis=0, keepdims=True) * (1.0 / patches)
        target = value * lax.rsqrt(spread + 1e-05)
        upper = target.astype(jnp.bfloat16)
        lower = (target - upper.astype(jnp.float32)).astype(jnp.bfloat16)
        kept = (jnp.dot(pick[...], upper, preferred_element_type=jnp.float32)
                + jnp.dot(pick[...], lower, preferred_element_type=jnp.float32))
        student = pf[q, :, y, z]
        for j in range(1, zs):
            student = student + h3r[j - 1, q].astype(jnp.float32)
        student = student.reshape(keep, LANE_BLOCK)
        ebuf[q, core, y, z] = ((student - kept) * (1.0 / math.sqrt(total_kept))).astype(jnp.bfloat16)
        for j in range(1, zs):
            error_level(q, j).start()

    def levels_in(q):
        for j in range(1, zs):
            ref = ebuf.at[q, core, y, lax.rem(z + zs - j, zs)]
            remote(ref, ref, zss.at[q, j - 1], zrs.at[q, j - 1], sibling).wait_recv()
        error_across(q, y).start()

    def across_in(q):
        error_across(q, 1 - y).wait_recv()
        error_sibling(q, core).start()

    def finish(q):
        error_sibling(q, other).wait_recv()
        total = None
        for g in range(2):
            errors = ebuf[q, :, :, :, g * part:(g + 1) * part].reshape(rows_core, LANE_BLOCK)
            term = jnp.dot(turned[g], errors, preferred_element_type=jnp.float32)
            total = term if total is None else total + term
        grad[:, q * LANE_BLOCK:(q + 1) * LANE_BLOCK] = total

    stages = (product, cores_add, error_of, levels_in, across_in, finish)
    for wave in range(blocks + len(stages) - 1):
        for lag, stage in enumerate(stages):
            if 0 <= wave - lag < blocks:
                stage(wave - lag)

    for copy in (stats, kept_out, halves, h1, h2):
        copy.wait_send()
    for q in range(blocks):
        for i in range(zs - 1):
            @pl.when((z > 0) & (z + i < zs))
            def _():
                line_copy(0, q, i, z, sibling).wait_send()

            @pl.when((z < zs - 1) & (z - i >= 0))
            def _():
                line_copy(1, q, i, z, sibling).wait_send()
        sibling_copy(q).wait_send()
        across_copy(q).wait_send()
        for j in range(1, zs):
            error_level(q, j).wait_send()
        error_across(q, y).wait_send()
        error_sibling(q, core).wait_send()
    for j in range(1, n):
        swap_copy(j).wait_send()
    for j in range(1, 4):
        feature_copy(0, j).wait_send()
    for j in range(4):
        feature_copy(1, j).wait_send()
    for j in range(1, zs):
        level_copy(j).wait_send()


def fused_shards(images, keep_index, teacher_weight, student_weight):
    n = lax.axis_size("fsdp")
    patches, width = images.shape[1:]
    keep = keep_index.shape[1]
    depth, columns = teacher_weight.shape
    zs, blocks, part = n // 4, columns // LANE_BLOCK, keep // 2
    pick = (keep_index[0][:, None] == jnp.arange(patches)[None, :]).astype(jnp.bfloat16)
    bf, fl = jnp.bfloat16, jnp.float32
    dma = pltpu.SemaphoreType.DMA
    vm = pltpu.VMEM
    scratch = [
        vm((patches, 128), fl), vm((patches, 128), fl),
        vm((2, 2, zs // 2, patches, depth), bf),
        vm((2, 2, zs, patches, depth), bf),
        vm((blocks, zs, depth, LANE_BLOCK), bf),
        vm((blocks, depth, LANE_BLOCK), bf),
        vm((blocks, 2, patches, LANE_BLOCK), fl),
        vm((blocks, 2, patches, LANE_BLOCK), fl),
        vm((blocks, 2, patches, LANE_BLOCK), fl),
        vm((blocks, patches, LANE_BLOCK), bf),
        vm((blocks, patches, LANE_BLOCK), bf),
        vm((n, part, depth), bf),
        vm((n // 2, part, depth), bf),
        vm((2, 2, 2, zs, part, depth), bf),
        vm((2, depth, n * part), bf),
        vm((blocks, 2, 2, zs, part, LANE_BLOCK), fl),
        vm((blocks, 2, 2, zs, part, LANE_BLOCK), bf),
        vm((blocks, 2, 2, zs, part, LANE_BLOCK), bf),
        vm((blocks, 2, zs, part, LANE_BLOCK), bf),
        vm((blocks, 2, zs, part, LANE_BLOCK), bf),
        vm((zs, blocks, 2, part, LANE_BLOCK), bf),
        vm((zs - 1, blocks, 2, part, LANE_BLOCK), bf),
        vm((blocks, 2, 2, zs, keep, LANE_BLOCK), bf),
        dma((1,)), dma((1,)),
        dma((2, 4)), dma((2, 4)),
        dma((2, blocks, zs - 1)), dma((2, blocks, zs - 1)),
        dma((1,)), dma((1,)),
        dma((n - 1,)), dma((n - 1,)),
        dma((1,)), dma((1,)), dma((1,)), dma((1,)), dma((1,)), dma((1,)),
        dma((zs - 1,)), dma((zs - 1,)),
        dma((blocks,)), dma((blocks,)), dma((blocks,)), dma((blocks,)),
        dma((blocks, zs - 1)), dma((blocks, zs - 1)),
        dma((blocks,)), dma((blocks,)), dma((blocks,)), dma((blocks,)),
    ]
    out = jax.ShapeDtypeStruct((depth, columns), fl)
    return pl.pallas_call(
        functools.partial(fused, n, keep * n),
        out_shape=(out, out),
        in_specs=[pl.BlockSpec(memory_space=pltpu.VMEM)] * 4,
        out_specs=(pl.BlockSpec(memory_space=pltpu.VMEM),) * 2,
        scratch_shapes=scratch,
        compiler_params=pltpu.CompilerParams(
            collective_id=0, has_side_effects=True, vmem_limit_bytes=60 * 2**20),
        cost_estimate=pl.CostEstimate(
            flops=2 * n * depth * columns * (patches + 2 * keep), bytes_accessed=2**24, transcendentals=0),
    )(pick, images[0], teacher_weight, student_weight)


def solution(mesh):
    placed = (P("fsdp", None, "tp"), P("fsdp", None), P("fsdp", "tp"), P("fsdp", "tp"))
    fits = mesh.shape["tp"] == 2 and mesh.shape["fsdp"] == 16
    return jax.shard_map(
        fused_shards if fits else shards,
        mesh=mesh,
        in_specs=placed,
        out_specs=(P("fsdp", "tp"), P("fsdp", "tp")),
        check_vma=False,
    )
```

```python
import functools
import math

import jax
import jax.numpy as jnp
from jax import lax
from jax.experimental import pallas as pl
from jax.experimental.pallas import tpu as pltpu
from jax.sharding import PartitionSpec as P

D = 6144


def layer_norm(values):
    floats = values.astype(jnp.float32)
    centre = jnp.mean(floats, axis=-1, keepdims=True)
    centred = floats - centre
    spread = jnp.mean(centred * centred, axis=-1, keepdims=True)
    return (centred * lax.rsqrt(spread + 1e-06)).astype(jnp.bfloat16)


def pick_rows(table, index):
    return jax.vmap(lambda block, rows: block[rows])(table, index)


def row_product(features, piece):
    return jnp.dot(features, piece, preferred_element_type=jnp.float32)


def whole_features(images):
    if lax.axis_size("tp") != 2:
        return lax.all_gather(images, "tp", axis=2, tiled=True)
    other = lax.ppermute(images, "tp", [(0, 1), (1, 0)])
    first = lax.axis_index("tp") == 0
    return jnp.concatenate(
        [jnp.where(first, images, other), jnp.where(first, other, images)], axis=2
    )


def shards(images, keep_index, teacher_weight, student_weight):
    img_count = images.shape[0]
    patch_count = images.shape[1]
    keep_count = keep_index.shape[1]
    columns_dev = teacher_weight.shape[1]
    teacher_next = 0.999 * teacher_weight + (1.0 - 0.999) * student_weight
    teacher_panel = teacher_next.astype(jnp.bfloat16)
    student_panel = student_weight.astype(jnp.bfloat16)
    whole_panel = lax.all_gather(teacher_panel, "fsdp", axis=0, tiled=True)
    normed = layer_norm(whole_features(images))
    flat_all = normed.reshape(img_count * patch_count, D)
    picked = pick_rows(normed, keep_index).reshape(img_count * keep_count, D)
    owned = lax.all_to_all(picked, "fsdp", split_axis=1, concat_axis=0, tiled=True)
    partial = row_product(owned, student_panel).astype(jnp.bfloat16)
    student_out = lax.psum_scatter(partial, "fsdp", scatter_dimension=0, tiled=True)
    student_out = student_out.astype(jnp.float32)
    teacher_out = row_product(flat_all, whole_panel)
    teacher_out = teacher_out.reshape(img_count, patch_count, columns_dev)
    centre = jnp.mean(teacher_out, axis=1, keepdims=True)
    centred_out = teacher_out - centre
    spread = jnp.mean(centred_out * centred_out, axis=1, keepdims=True)
    target = centred_out * lax.rsqrt(spread + 1e-05)
    target_kept = pick_rows(target, keep_index).reshape(img_count * keep_count, columns_dev)
    total_kept = img_count * keep_count * lax.axis_size("fsdp")
    error = ((student_out - target_kept) * (1.0 / math.sqrt(total_kept))).astype(jnp.bfloat16)
    student_grad = lax.dot_general(
        owned,
        lax.all_gather(error, "fsdp", axis=0, tiled=True),
        (((0,), (0,)), ((), ())),
        preferred_element_type=jnp.float32,
    )
    return (teacher_next, student_grad)


MESH = pl.DeviceIdType.MESH
LANE_BLOCK = 256


def fused(n, total_kept, pick, images_hbm, tw_hbm, sw_hbm, tnext_hbm, grad_hbm, images, tw, sw, tnext, grad, stat, stat_in, nbuf, xk, wt, ws,
          pt, os_, or_, ys_, yr_, pb, pxs, owned, turned, pf, h1s, h1r, h2s, h2r, h3s, h3r, ebuf,
          sts, str_, xs, xr, ls, lr, ps, pr, as_, ar, ss, sr, h1ss, h1rs, h2ss, h2rs, h3ss, h3rs,
          oss, ors, yss, yrs, zss, zrs, ess, ers, bss, brs, loads, stores):
    f = lax.axis_index("fsdp")
    t = lax.axis_index("tp")
    zs = n // 4
    side = n // 2
    z = lax.div(f, 4)
    spot = lax.rem(f, 4)
    y = lax.div(spot, 2)
    core = lax.rem(spot, 2)
    other = 1 - core
    patches, width = images.shape
    depth = tw.shape[0]
    blocks = tw.shape[1] // LANE_BLOCK
    keep = pick.shape[0]
    part = keep // 2
    sibling = (4 * z + 2 * y + other, t)
    across = (4 * z + 2 * (1 - y) + core, t)
    mirror = (f, 1 - t)

    def remote(src, dst, send, recv, device):
        return pltpu.make_async_remote_copy(
            src_ref=src, dst_ref=dst, send_sem=send, recv_sem=recv,
            device_id=device, device_id_type=MESH)

    fetched = [pltpu.make_async_copy(a, b, loads.at[i])
               for i, (a, b) in enumerate(((tw_hbm, tw), (sw_hbm, sw), (images_hbm, images)))]
    for copy in fetched:
        copy.start()

    barrier = pltpu.get_barrier_semaphore()
    for j in range(1, n):
        pl.semaphore_signal(barrier, inc=1, device_id=(lax.rem(f + j, n), t), device_id_type=MESH)
    for j in range(4):
        pl.semaphore_signal(
            barrier, inc=1, device_id=(4 * z + lax.rem(spot + j, 4), 1 - t), device_id_type=MESH)
    pl.semaphore_wait(barrier, n + 3)

    def line_copy(way, q, i, source, to):
        ref = wt.at[q, source]
        return remote(ref, ref, ls.at[way, q, i], lr.at[way, q, i], to)

    down = (f - 4, t)
    up = (f + 4, t)
    tile = 64
    fetched[0].wait()
    fetched[1].wait()
    for q in range(blocks):
        columns = slice(q * LANE_BLOCK, (q + 1) * LANE_BLOCK)

        @pl.loop(0, depth // tile)
        def _(i):
            rows = pl.ds(pl.multiple_of(i * tile, tile), tile)
            student = sw[rows, columns]
            following = 0.999 * tw[rows, columns] + (1.0 - 0.999) * student
            tnext[rows, columns] = following
            wt[q, z, rows, :] = following.astype(jnp.bfloat16)
            ws[q, rows, :] = student.astype(jnp.bfloat16)

        @pl.when(z > 0)
        def _():
            line_copy(0, q, 0, z, down).start()

        @pl.when(z < zs - 1)
        def _():
            line_copy(1, q, 0, z, up).start()

    next_out = pltpu.make_async_copy(tnext, tnext_hbm, stores.at[blocks])
    next_out.start()

    fetched[2].wait()
    lane = lax.broadcasted_iota(jnp.int32, (16, 128), 1)

    @pl.loop(0, patches // 16)
    def _(i):
        rows = pl.ds(pl.multiple_of(i * 16, 16), 16)
        values = images[rows, :].astype(jnp.float32)
        centre = jnp.sum(values, axis=1, keepdims=True) * (1.0 / width)
        values = values - centre
        spread = jnp.sum(values * values, axis=1, keepdims=True)
        stat[rows, :] = jnp.where(lane < 64, centre, spread)

    stats = remote(stat, stat_in, sts.at[0], str_.at[0], mirror)
    stats.start()

    def pump(i, q):
        @pl.when(z + 1 + i < zs)
        def _():
            line_copy(0, q, i, z + 1 + i, sibling).wait_recv()
            if i < zs - 2:
                @pl.when(z > 0)
                def _():
                    line_copy(0, q, i + 1, z + 1 + i, down).start()

        @pl.when(z - 1 - i >= 0)
        def _():
            line_copy(1, q, i, z - 1 - i, sibling).wait_recv()
            if i < zs - 2:
                @pl.when(z < zs - 1)
                def _():
                    line_copy(1, q, i + 1, z - 1 - i, up).start()

    stats.wait_recv()

    @pl.loop(0, patches // 16)
    def _(i):
        rows = pl.ds(pl.multiple_of(i * 16, 16), 16)
        here, there = stat[rows, :], stat_in[rows, :]
        centre = (here[:, 0:1] + there[:, 0:1]) * 0.5
        apart = here[:, 0:1] - there[:, 0:1]
        spread = (here[:, 64:65] + there[:, 64:65]) * (0.5 / width) + apart * apart * 0.25
        scaled = ((images[rows, :].astype(jnp.float32) - centre) * lax.rsqrt(spread + 1e-06)).astype(jnp.bfloat16)
        for j in range(side):
            nbuf[j % 4 // 2, j % 2, j // 4, rows, :] = scaled[:, j * depth:(j + 1) * depth]

    @pl.loop(0, side // 4)
    def _(level):
        for j in range(4):
            rows = jnp.dot(pick[...], nbuf[j // 2, j % 2, level],
                           preferred_element_type=jnp.float32).astype(jnp.bfloat16)
            pb[side * t + 4 * level + j] = rows[:part]
            pxs[4 * level + j] = rows[part:]

    kept_out = remote(pxs, pb.at[pl.ds(side * t, side)], ps.at[0], pr.at[0], mirror)
    kept_out.start()

    def feature_copy(plane, j):
        to = lax.rem(spot + j, 4)
        return remote(nbuf.at[lax.div(to, 2), lax.rem(to, 2)], xk.at[y, core, pl.ds(2 * t, 2)],
                      xs.at[plane, j], xr.at[plane, j],
                      (4 * z + to, t if plane == 0 else 1 - t))

    xk[y, core, pl.ds(2 * t, 2)] = nbuf[y, core]
    kept_in = remote(pxs, pb.at[pl.ds(side * (1 - t), side)], ps.at[0], pr.at[0], mirror)
    kept_in.wait_recv()

    def half_of(device):
        return lax.rem(t + lax.div(device, side), 2)

    def swap_copy(j):
        to = lax.rem(f + j, n)
        return remote(pb.at[to], owned.at[half_of(to), core, y, z], as_.at[j - 1], ar.at[j - 1], (to, t))

    mine = half_of(f)
    for j in range(1, n):
        swap_copy(j).start()
    owned[mine, core, y, z] = pb[f]
    for j in range(1, 4):
        feature_copy(0, j).start()
    for j in range(2):
        feature_copy(1, j).start()

    for q in range(blocks // 2):
        pump(0, q)

    for j in range(1, n):
        origin = lax.rem(f + n - j, n)
        remote(pb.at[0],
               owned.at[mine, lax.rem(origin, 2), lax.div(lax.rem(origin, 4), 2), lax.div(origin, 4)],
               as_.at[j - 1], ar.at[j - 1], (origin, t)).wait_recv()
    halves = remote(owned.at[mine], owned.at[mine], ss.at[0], sr.at[0], mirror)
    halves.start()
    for j in range(2, 4):
        feature_copy(1, j).start()
    for q in range(blocks // 2, blocks):
        pump(0, q)
    remote(owned.at[1 - mine], owned.at[1 - mine], ss.at[0], sr.at[0], mirror).wait_recv()

    split = (2, 2, zs, part, LANE_BLOCK)
    rows_core = 4 * zs * part

    def h1_copy(q):
        return remote(h1s.at[q], h1r.at[q], h1ss.at[q], h1rs.at[q], sibling)

    def h2_copy(q):
        return remote(h2s.at[q], h2r.at[q], h2ss.at[q], h2rs.at[q], across)

    def level_copy(q, j):
        to = lax.rem(z + j, zs)
        return remote(h3s.at[q, to], h3r.at[q, j - 1], h3ss.at[q, j - 1], h3rs.at[q, j - 1], (4 * to + spot, t))

    @pl.loop(0, blocks)
    def _(q):
        panel = ws[q]
        send = jnp.dot(owned[:, other].reshape(rows_core, depth), panel,
                       preferred_element_type=jnp.float32)
        h1s[q] = send.astype(jnp.bfloat16).reshape(split)
        h1_copy(q).start()
        own = jnp.dot(owned[:, core].reshape(rows_core, depth), panel,
                      preferred_element_type=jnp.float32)
        pf[q] = own.reshape(split)

    @pl.loop(0, blocks)
    def _(q):
        h1_copy(q).wait_recv()
        for g in range(2):
            h2s[q, g] = (pf[q, g, 1 - y] + h1r[q, g, 1 - y].astype(jnp.float32)).astype(jnp.bfloat16)
            pf[q, g, y] += h1r[q, g, y].astype(jnp.float32)
        h2_copy(q).start()

    for g in range(2):
        turned[g] = owned[g].reshape(rows_core, depth).T

    for q in range(blocks):
        pump(1, q)
        h2_copy(q).wait_recv()

        @pl.loop(0, zs)
        def _(level):
            for g in range(2):
                value = pf[q, g, y, level] + h2r[q, g, level].astype(jnp.float32)
                pf[q, g, y, level] = value
                h3s[q, level, g] = value.astype(jnp.bfloat16)

        for j in range(1, zs):
            level_copy(q, j).start()

    def feature_wait(plane, j):
        origin = lax.rem(spot + 4 - j, 4)
        first = 2 * t if plane == 0 else 2 * (1 - t)
        remote(nbuf.at[0, 0], xk.at[lax.div(origin, 2), lax.rem(origin, 2), pl.ds(first, 2)],
               xs.at[plane, j], xr.at[plane, j], sibling).wait_recv()

    for j in range(1, 4):
        feature_wait(0, j)
    for j in range(4):
        feature_wait(1, j)

    def sibling_copy(q):
        return remote(os_.at[q], or_.at[q], oss.at[q], ors.at[q], sibling)

    def across_copy(q):
        return remote(ys_.at[q], yr_.at[q], yss.at[q], yrs.at[q], across)

    def error_level(q, j):
        ref = ebuf.at[q, core, y, z]
        return remote(ref, ref, zss.at[q, j - 1], zrs.at[q, j - 1], (4 * lax.rem(z + j, zs) + spot, t))

    def error_across(q, row):
        ref = ebuf.at[q, core, row]
        return remote(ref, ref, ess.at[q], ers.at[q], across)

    def error_sibling(q, owner):
        ref = ebuf.at[q, owner]
        return remote(ref, ref, bss.at[q], brs.at[q], sibling)

    def product(q):
        if zs > 2:
            pump(zs - 2, q)

        @pl.loop(0, 2)
        def _(row):
            for target, owner in ((os_, other), (pt, core)):
                total = jnp.dot(xk[row, owner, 0], wt[q, 0], preferred_element_type=jnp.float32)
                for level in range(1, zs):
                    total += jnp.dot(xk[row, owner, level], wt[q, level],
                                     preferred_element_type=jnp.float32)
                target[q, row] = total

        sibling_copy(q).start()

    def cores_add(q):
        sibling_copy(q).wait_recv()
        ys_[q] = (pt[q, 1 - y] + or_[q, 1 - y]).astype(jnp.bfloat16)
        across_copy(q).start()
        pt[q, y] += or_[q, y]

    def error_of(q):
        for j in range(1, zs):
            level_copy(q, j).wait_recv()
        across_copy(q).wait_recv()
        value = pt[q, y] + yr_[q].astype(jnp.float32)
        centre = jnp.sum(value, axis=0, keepdims=True) * (1.0 / patches)
        value = value - centre
        spread = jnp.sum(value * value, axis=0, keepdims=True) * (1.0 / patches)
        target = value * lax.rsqrt(spread + 1e-05)
        upper = target.astype(jnp.bfloat16)
        lower = (target - upper.astype(jnp.float32)).astype(jnp.bfloat16)
        kept = (jnp.dot(pick[...], upper, preferred_element_type=jnp.float32)
                + jnp.dot(pick[...], lower, preferred_element_type=jnp.float32))
        student = pf[q, :, y, z]
        for j in range(1, zs):
            student = student + h3r[q, j - 1].astype(jnp.float32)
        student = student.reshape(keep, LANE_BLOCK)
        ebuf[q, core, y, z] = ((student - kept) * (1.0 / math.sqrt(total_kept))).astype(jnp.bfloat16)
        for j in range(1, zs):
            error_level(q, j).start()

    def levels_in(q):
        for j in range(1, zs):
            ref = ebuf.at[q, core, y, lax.rem(z + zs - j, zs)]
            remote(ref, ref, zss.at[q, j - 1], zrs.at[q, j - 1], sibling).wait_recv()
        error_across(q, y).start()

    def across_in(q):
        error_across(q, 1 - y).wait_recv()
        error_sibling(q, core).start()

    def finish(q):
        error_sibling(q, other).wait_recv()
        total = None
        for g in range(2):
            errors = ebuf[q, :, :, :, g * part:(g + 1) * part].reshape(rows_core, LANE_BLOCK)
            term = jnp.dot(turned[g], errors, preferred_element_type=jnp.float32)
            total = term if total is None else total + term
        grad[:, q * LANE_BLOCK:(q + 1) * LANE_BLOCK] = total
        grad_copy(q).start()

    def grad_copy(q):
        columns = pl.ds(q * LANE_BLOCK, LANE_BLOCK)
        return pltpu.make_async_copy(grad.at[:, columns], grad_hbm.at[:, columns], stores.at[q])

    stages = ((product, 0), (error_of, 1), (cores_add, 0), (levels_in, 2), (across_in, 3), (finish, 4))
    for wave in range(blocks + 4):
        for stage, lag in stages:
            if 0 <= wave - lag < blocks:
                stage(wave - lag)

    for copy in (stats, kept_out, halves):
        copy.wait_send()
    next_out.wait()
    for q in range(blocks):
        for i in range(zs - 1):
            @pl.when((z > 0) & (z + i < zs))
            def _():
                line_copy(0, q, i, z, sibling).wait_send()

            @pl.when((z < zs - 1) & (z - i >= 0))
            def _():
                line_copy(1, q, i, z, sibling).wait_send()
        grad_copy(q).wait()
        h1_copy(q).wait_send()
        h2_copy(q).wait_send()
        sibling_copy(q).wait_send()
        across_copy(q).wait_send()
        for j in range(1, zs):
            level_copy(q, j).wait_send()
            error_level(q, j).wait_send()
        error_across(q, y).wait_send()
        error_sibling(q, core).wait_send()
    for j in range(1, n):
        swap_copy(j).wait_send()
    for j in range(1, 4):
        feature_copy(0, j).wait_send()
    for j in range(4):
        feature_copy(1, j).wait_send()


def fused_shards(images, keep_index, teacher_weight, student_weight):
    n = lax.axis_size("fsdp")
    patches, width = images.shape[1:]
    keep = keep_index.shape[1]
    depth, columns = teacher_weight.shape
    zs, blocks, part = n // 4, columns // LANE_BLOCK, keep // 2
    pick = (keep_index[0][:, None] == jnp.arange(patches)[None, :]).astype(jnp.bfloat16)
    bf, fl = jnp.bfloat16, jnp.float32
    dma = pltpu.SemaphoreType.DMA
    vm = pltpu.VMEM
    scratch = [
        vm((patches, width), bf), vm((depth, columns), fl), vm((depth, columns), fl),
        vm((depth, columns), fl), vm((depth, columns), fl),
        vm((patches, 128), fl), vm((patches, 128), fl),
        vm((2, 2, zs // 2, patches, depth), bf),
        vm((2, 2, zs, patches, depth), bf),
        vm((blocks, zs, depth, LANE_BLOCK), bf),
        vm((blocks, depth, LANE_BLOCK), bf),
        vm((blocks, 2, patches, LANE_BLOCK), fl),
        vm((blocks, 2, patches, LANE_BLOCK), fl),
        vm((blocks, 2, patches, LANE_BLOCK), fl),
        vm((blocks, patches, LANE_BLOCK), bf),
        vm((blocks, patches, LANE_BLOCK), bf),
        vm((n, part, depth), bf),
        vm((n // 2, part, depth), bf),
        vm((2, 2, 2, zs, part, depth), bf),
        vm((2, depth, n * part), bf),
        vm((blocks, 2, 2, zs, part, LANE_BLOCK), fl),
        vm((blocks, 2, 2, zs, part, LANE_BLOCK), bf),
        vm((blocks, 2, 2, zs, part, LANE_BLOCK), bf),
        vm((blocks, 2, zs, part, LANE_BLOCK), bf),
        vm((blocks, 2, zs, part, LANE_BLOCK), bf),
        vm((blocks, zs, 2, part, LANE_BLOCK), bf),
        vm((blocks, zs - 1, 2, part, LANE_BLOCK), bf),
        vm((blocks, 2, 2, zs, keep, LANE_BLOCK), bf),
        dma((1,)), dma((1,)),
        dma((2, 4)), dma((2, 4)),
        dma((2, blocks, zs - 1)), dma((2, blocks, zs - 1)),
        dma((1,)), dma((1,)),
        dma((n - 1,)), dma((n - 1,)),
        dma((1,)), dma((1,)),
        dma((blocks,)), dma((blocks,)), dma((blocks,)), dma((blocks,)),
        dma((blocks, zs - 1)), dma((blocks, zs - 1)),
        dma((blocks,)), dma((blocks,)), dma((blocks,)), dma((blocks,)),
        dma((blocks, zs - 1)), dma((blocks, zs - 1)),
        dma((blocks,)), dma((blocks,)), dma((blocks,)), dma((blocks,)),
        dma((3,)), dma((blocks + 1,)),
    ]
    out = jax.ShapeDtypeStruct((depth, columns), fl)
    return pl.pallas_call(
        functools.partial(fused, n, keep * n),
        out_shape=(out, out),
        in_specs=[pl.BlockSpec(memory_space=pltpu.VMEM)] + [pl.BlockSpec(memory_space=pl.ANY)] * 3,
        out_specs=(pl.BlockSpec(memory_space=pl.ANY),) * 2,
        scratch_shapes=scratch,
        compiler_params=pltpu.CompilerParams(
            collective_id=0, has_side_effects=True, vmem_limit_bytes=60 * 2**20),
        cost_estimate=pl.CostEstimate(
            flops=2 * n * depth * columns * (patches + 2 * keep), bytes_accessed=2**24, transcendentals=0),
    )(pick, images[0], teacher_weight, student_weight)


def solution(mesh):
    placed = (P("fsdp", None, "tp"), P("fsdp", None), P("fsdp", "tp"), P("fsdp", "tp"))
    fits = mesh.shape["tp"] == 2 and mesh.shape["fsdp"] == 16
    return jax.shard_map(
        fused_shards if fits else shards,
        mesh=mesh,
        in_specs=placed,
        out_specs=(P("fsdp", "tp"), P("fsdp", "tp")),
        check_vma=False,
    )
```

```python
import functools
import math

import jax
import jax.numpy as jnp
from jax import lax
from jax.experimental import pallas as pl
from jax.experimental.pallas import tpu as pltpu
from jax.sharding import PartitionSpec as P

D = 6144


def layer_norm(values):
    floats = values.astype(jnp.float32)
    centre = jnp.mean(floats, axis=-1, keepdims=True)
    centred = floats - centre
    spread = jnp.mean(centred * centred, axis=-1, keepdims=True)
    return (centred * lax.rsqrt(spread + 1e-06)).astype(jnp.bfloat16)


def pick_rows(table, index):
    return jax.vmap(lambda block, rows: block[rows])(table, index)


def row_product(features, piece):
    return jnp.dot(features, piece, preferred_element_type=jnp.float32)


def whole_features(images):
    if lax.axis_size("tp") != 2:
        return lax.all_gather(images, "tp", axis=2, tiled=True)
    other = lax.ppermute(images, "tp", [(0, 1), (1, 0)])
    first = lax.axis_index("tp") == 0
    return jnp.concatenate(
        [jnp.where(first, images, other), jnp.where(first, other, images)], axis=2
    )


def shards(images, keep_index, teacher_weight, student_weight):
    img_count = images.shape[0]
    patch_count = images.shape[1]
    keep_count = keep_index.shape[1]
    columns_dev = teacher_weight.shape[1]
    teacher_next = 0.999 * teacher_weight + (1.0 - 0.999) * student_weight
    teacher_panel = teacher_next.astype(jnp.bfloat16)
    student_panel = student_weight.astype(jnp.bfloat16)
    whole_panel = lax.all_gather(teacher_panel, "fsdp", axis=0, tiled=True)
    normed = layer_norm(whole_features(images))
    flat_all = normed.reshape(img_count * patch_count, D)
    picked = pick_rows(normed, keep_index).reshape(img_count * keep_count, D)
    owned = lax.all_to_all(picked, "fsdp", split_axis=1, concat_axis=0, tiled=True)
    partial = row_product(owned, student_panel).astype(jnp.bfloat16)
    student_out = lax.psum_scatter(partial, "fsdp", scatter_dimension=0, tiled=True)
    student_out = student_out.astype(jnp.float32)
    teacher_out = row_product(flat_all, whole_panel)
    teacher_out = teacher_out.reshape(img_count, patch_count, columns_dev)
    centre = jnp.mean(teacher_out, axis=1, keepdims=True)
    centred_out = teacher_out - centre
    spread = jnp.mean(centred_out * centred_out, axis=1, keepdims=True)
    target = centred_out * lax.rsqrt(spread + 1e-05)
    target_kept = pick_rows(target, keep_index).reshape(img_count * keep_count, columns_dev)
    total_kept = img_count * keep_count * lax.axis_size("fsdp")
    error = ((student_out - target_kept) * (1.0 / math.sqrt(total_kept))).astype(jnp.bfloat16)
    student_grad = lax.dot_general(
        owned,
        lax.all_gather(error, "fsdp", axis=0, tiled=True),
        (((0,), (0,)), ((), ())),
        preferred_element_type=jnp.float32,
    )
    return (teacher_next, student_grad)


MESH = pl.DeviceIdType.MESH
LANE_BLOCK = 256


def fused(n, total_kept, pick, images_hbm, tw_hbm, sw_hbm, tnext_hbm, grad_hbm, images, tw, sw, tnext, grad, stat, stat_in, nbuf, xk, wt, ws,
          pt, os_, or_, ys_, yr_, pb, pxs, owned, turned, pf, h1s, h1r, h2s, h2r, h3s, h3r, ebuf,
          sts, str_, xs, xr, ls, lr, ps, pr, as_, ar, ss, sr, h1ss, h1rs, h2ss, h2rs, h3ss, h3rs,
          oss, ors, yss, yrs, zss, zrs, ess, ers, bss, brs, loads, stores):
    f = lax.axis_index("fsdp")
    t = lax.axis_index("tp")
    zs = n // 4
    side = n // 2
    z = lax.div(f, 4)
    spot = lax.rem(f, 4)
    y = lax.div(spot, 2)
    core = lax.rem(spot, 2)
    other = 1 - core
    patches, width = images.shape
    depth = tw.shape[0]
    blocks = tw.shape[1] // LANE_BLOCK
    keep = pick.shape[0]
    part = keep // 2
    sibling = (4 * z + 2 * y + other, t)
    across = (4 * z + 2 * (1 - y) + core, t)
    mirror = (f, 1 - t)

    def remote(src, dst, send, recv, device):
        return pltpu.make_async_remote_copy(
            src_ref=src, dst_ref=dst, send_sem=send, recv_sem=recv,
            device_id=device, device_id_type=MESH)

    fetched = [pltpu.make_async_copy(a, b, loads.at[i])
               for i, (a, b) in enumerate(((tw_hbm, tw), (sw_hbm, sw), (images_hbm, images)))]
    for copy in fetched:
        copy.start()

    barrier = pltpu.get_barrier_semaphore()
    for j in range(1, n):
        pl.semaphore_signal(barrier, inc=1, device_id=(lax.rem(f + j, n), t), device_id_type=MESH)
    for j in range(4):
        pl.semaphore_signal(
            barrier, inc=1, device_id=(4 * z + lax.rem(spot + j, 4), 1 - t), device_id_type=MESH)
    pl.semaphore_wait(barrier, n + 3)

    def line_copy(way, q, i, source, to):
        ref = wt.at[q, source]
        return remote(ref, ref, ls.at[way, q, i], lr.at[way, q, i], to)

    down = (f - 4, t)
    up = (f + 4, t)
    tile = 64
    fetched[0].wait()
    fetched[1].wait()
    def panel_block(q):
        columns = slice(q * LANE_BLOCK, (q + 1) * LANE_BLOCK)

        @pl.loop(0, depth // tile)
        def _(i):
            rows = pl.ds(pl.multiple_of(i * tile, tile), tile)
            student = sw[rows, columns]
            following = 0.999 * tw[rows, columns] + (1.0 - 0.999) * student
            tnext[rows, columns] = following
            wt[q, z, rows, :] = following.astype(jnp.bfloat16)
            ws[q, rows, :] = student.astype(jnp.bfloat16)

    def send_block(q):
        @pl.when(z > 0)
        def _():
            line_copy(0, q, 0, z, down).start()

        @pl.when(z < zs - 1)
        def _():
            line_copy(1, q, 0, z, up).start()

    early = blocks // 2
    for q in range(early):
        panel_block(q)
        send_block(q)

    fetched[2].wait()
    lane = lax.broadcasted_iota(jnp.int32, (16, 128), 1)

    @pl.loop(0, patches // 16)
    def _(i):
        rows = pl.ds(pl.multiple_of(i * 16, 16), 16)
        values = images[rows, :].astype(jnp.float32)
        centre = jnp.sum(values, axis=1, keepdims=True) * (1.0 / width)
        values = values - centre
        spread = jnp.sum(values * values, axis=1, keepdims=True)
        stat[rows, :] = jnp.where(lane < 64, centre, spread)

    stats = remote(stat, stat_in, sts.at[0], str_.at[0], mirror)
    stats.start()

    for q in range(early, blocks):
        panel_block(q)
    next_out = pltpu.make_async_copy(tnext, tnext_hbm, stores.at[blocks])
    next_out.start()

    def pump(i, q):
        @pl.when(z + 1 + i < zs)
        def _():
            line_copy(0, q, i, z + 1 + i, sibling).wait_recv()
            if i < zs - 2:
                @pl.when(z > 0)
                def _():
                    line_copy(0, q, i + 1, z + 1 + i, down).start()

        @pl.when(z - 1 - i >= 0)
        def _():
            line_copy(1, q, i, z - 1 - i, sibling).wait_recv()
            if i < zs - 2:
                @pl.when(z < zs - 1)
                def _():
                    line_copy(1, q, i + 1, z - 1 - i, up).start()

    stats.wait_recv()

    @pl.loop(0, patches // 16)
    def _(i):
        rows = pl.ds(pl.multiple_of(i * 16, 16), 16)
        here, there = stat[rows, :], stat_in[rows, :]
        centre = (here[:, 0:1] + there[:, 0:1]) * 0.5
        apart = here[:, 0:1] - there[:, 0:1]
        spread = (here[:, 64:65] + there[:, 64:65]) * (0.5 / width) + apart * apart * 0.25
        scaled = ((images[rows, :].astype(jnp.float32) - centre) * lax.rsqrt(spread + 1e-06)).astype(jnp.bfloat16)
        for j in range(side):
            nbuf[j % 4 // 2, j % 2, j // 4, rows, :] = scaled[:, j * depth:(j + 1) * depth]

    @pl.loop(0, side // 4)
    def _(level):
        for j in range(4):
            rows = jnp.dot(pick[...], nbuf[j // 2, j % 2, level],
                           preferred_element_type=jnp.float32).astype(jnp.bfloat16)
            pb[side * t + 4 * level + j] = rows[:part]
            pxs[4 * level + j] = rows[part:]

    kept_out = remote(pxs, pb.at[pl.ds(side * t, side)], ps.at[0], pr.at[0], mirror)
    kept_out.start()

    def feature_copy(plane, j):
        to = lax.rem(spot + j, 4)
        return remote(nbuf.at[lax.div(to, 2), lax.rem(to, 2)], xk.at[y, core, pl.ds(2 * t, 2)],
                      xs.at[plane, j], xr.at[plane, j],
                      (4 * z + to, t if plane == 0 else 1 - t))

    xk[y, core, pl.ds(2 * t, 2)] = nbuf[y, core]
    kept_in = remote(pxs, pb.at[pl.ds(side * (1 - t), side)], ps.at[0], pr.at[0], mirror)
    kept_in.wait_recv()

    def half_of(device):
        return lax.rem(t + lax.div(device, side), 2)

    def swap_copy(j):
        to = lax.rem(f + j, n)
        return remote(pb.at[to], owned.at[half_of(to), core, y, z], as_.at[j - 1], ar.at[j - 1], (to, t))

    mine = half_of(f)
    for j in range(1, n):
        swap_copy(j).start()
    for q in range(early, blocks):
        send_block(q)
    owned[mine, core, y, z] = pb[f]
    for j in range(1, 4):
        feature_copy(0, j).start()
    for j in range(2):
        feature_copy(1, j).start()

    for q in range(blocks // 2):
        pump(0, q)

    for j in range(1, n):
        origin = lax.rem(f + n - j, n)
        remote(pb.at[0],
               owned.at[mine, lax.rem(origin, 2), lax.div(lax.rem(origin, 4), 2), lax.div(origin, 4)],
               as_.at[j - 1], ar.at[j - 1], (origin, t)).wait_recv()
    halves = remote(owned.at[mine], owned.at[mine], ss.at[0], sr.at[0], mirror)
    halves.start()
    for j in range(2, 4):
        feature_copy(1, j).start()
    for q in range(blocks // 2, blocks):
        pump(0, q)
    remote(owned.at[1 - mine], owned.at[1 - mine], ss.at[0], sr.at[0], mirror).wait_recv()

    split = (2, 2, zs, part, LANE_BLOCK)
    rows_core = 4 * zs * part

    def h1_copy(q):
        return remote(h1s.at[q], h1r.at[q], h1ss.at[q], h1rs.at[q], sibling)

    def h2_copy(q):
        return remote(h2s.at[q], h2r.at[q], h2ss.at[q], h2rs.at[q], across)

    def level_copy(q, j):
        to = lax.rem(z + j, zs)
        return remote(h3s.at[q, to], h3r.at[q, j - 1], h3ss.at[q, j - 1], h3rs.at[q, j - 1], (4 * to + spot, t))

    @pl.loop(0, blocks)
    def _(q):
        panel = ws[q]
        send = jnp.dot(owned[:, other].reshape(rows_core, depth), panel,
                       preferred_element_type=jnp.float32)
        h1s[q] = send.astype(jnp.bfloat16).reshape(split)
        h1_copy(q).start()
        own = jnp.dot(owned[:, core].reshape(rows_core, depth), panel,
                      preferred_element_type=jnp.float32)
        pf[q] = own.reshape(split)

    @pl.loop(0, blocks)
    def _(q):
        h1_copy(q).wait_recv()
        for g in range(2):
            h2s[q, g] = (pf[q, g, 1 - y] + h1r[q, g, 1 - y].astype(jnp.float32)).astype(jnp.bfloat16)
            pf[q, g, y] += h1r[q, g, y].astype(jnp.float32)
        h2_copy(q).start()

    for g in range(2):
        turned[g] = owned[g].reshape(rows_core, depth).T

    for q in range(blocks):
        pump(1, q)
        h2_copy(q).wait_recv()

        @pl.loop(0, zs)
        def _(level):
            for g in range(2):
                value = pf[q, g, y, level] + h2r[q, g, level].astype(jnp.float32)
                pf[q, g, y, level] = value
                h3s[q, level, g] = value.astype(jnp.bfloat16)

        for j in range(1, zs):
            level_copy(q, j).start()

    def feature_wait(plane, j):
        origin = lax.rem(spot + 4 - j, 4)
        first = 2 * t if plane == 0 else 2 * (1 - t)
        remote(nbuf.at[0, 0], xk.at[lax.div(origin, 2), lax.rem(origin, 2), pl.ds(first, 2)],
               xs.at[plane, j], xr.at[plane, j], sibling).wait_recv()

    for j in range(1, 4):
        feature_wait(0, j)
    for j in range(4):
        feature_wait(1, j)

    def sibling_copy(q):
        return remote(os_.at[q], or_.at[q], oss.at[q], ors.at[q], sibling)

    def across_copy(q):
        return remote(ys_.at[q], yr_.at[q], yss.at[q], yrs.at[q], across)

    def error_level(q, j):
        ref = ebuf.at[q, core, y, z]
        return remote(ref, ref, zss.at[q, j - 1], zrs.at[q, j - 1], (4 * lax.rem(z + j, zs) + spot, t))

    def error_across(q, row):
        ref = ebuf.at[q, core, row]
        return remote(ref, ref, ess.at[q], ers.at[q], across)

    def error_sibling(q, owner):
        ref = ebuf.at[q, owner]
        return remote(ref, ref, bss.at[q], brs.at[q], sibling)

    def product(q):
        if zs > 2:
            pump(zs - 2, q)

        @pl.loop(0, 2)
        def _(row):
            for target, owner in ((os_, other), (pt, core)):
                total = jnp.dot(xk[row, owner, 0], wt[q, 0], preferred_element_type=jnp.float32)
                for level in range(1, zs):
                    total += jnp.dot(xk[row, owner, level], wt[q, level],
                                     preferred_element_type=jnp.float32)
                target[q, row] = total

        sibling_copy(q).start()

    def cores_add(q):
        sibling_copy(q).wait_recv()
        ys_[q] = (pt[q, 1 - y] + or_[q, 1 - y]).astype(jnp.bfloat16)
        across_copy(q).start()
        pt[q, y] += or_[q, y]

    def error_of(q):
        for j in range(1, zs):
            level_copy(q, j).wait_recv()
        across_copy(q).wait_recv()
        value = pt[q, y] + yr_[q].astype(jnp.float32)
        centre = jnp.sum(value, axis=0, keepdims=True) * (1.0 / patches)
        value = value - centre
        spread = jnp.sum(value * value, axis=0, keepdims=True) * (1.0 / patches)
        target = value * lax.rsqrt(spread + 1e-05)
        upper = target.astype(jnp.bfloat16)
        lower = (target - upper.astype(jnp.float32)).astype(jnp.bfloat16)
        kept = (jnp.dot(pick[...], upper, preferred_element_type=jnp.float32)
                + jnp.dot(pick[...], lower, preferred_element_type=jnp.float32))
        student = pf[q, :, y, z]
        for j in range(1, zs):
            student = student + h3r[q, j - 1].astype(jnp.float32)
        student = student.reshape(keep, LANE_BLOCK)
        ebuf[q, core, y, z] = ((student - kept) * (1.0 / math.sqrt(total_kept))).astype(jnp.bfloat16)
        for j in range(1, zs):
            error_level(q, j).start()

    def levels_in(q):
        for j in range(1, zs):
            ref = ebuf.at[q, core, y, lax.rem(z + zs - j, zs)]
            remote(ref, ref, zss.at[q, j - 1], zrs.at[q, j - 1], sibling).wait_recv()
        error_across(q, y).start()

    def across_in(q):
        error_across(q, 1 - y).wait_recv()
        error_sibling(q, core).start()

    def finish(q):
        error_sibling(q, other).wait_recv()
        total = None
        for g in range(2):
            errors = ebuf[q, :, :, :, g * part:(g + 1) * part].reshape(rows_core, LANE_BLOCK)
            term = jnp.dot(turned[g], errors, preferred_element_type=jnp.float32)
            total = term if total is None else total + term
        grad[:, q * LANE_BLOCK:(q + 1) * LANE_BLOCK] = total
        grad_copy(q).start()

    def grad_copy(q):
        columns = pl.ds(q * LANE_BLOCK, LANE_BLOCK)
        return pltpu.make_async_copy(grad.at[:, columns], grad_hbm.at[:, columns], stores.at[q])

    stages = ((product, 0), (error_of, 1), (cores_add, 0), (levels_in, 2), (across_in, 3), (finish, 4))
    for wave in range(blocks + 4):
        for stage, lag in stages:
            if 0 <= wave - lag < blocks:
                stage(wave - lag)

    for copy in (stats, kept_out, halves):
        copy.wait_send()
    next_out.wait()
    for q in range(blocks):
        for i in range(zs - 1):
            @pl.when((z > 0) & (z + i < zs))
            def _():
                line_copy(0, q, i, z, sibling).wait_send()

            @pl.when((z < zs - 1) & (z - i >= 0))
            def _():
                line_copy(1, q, i, z, sibling).wait_send()
        grad_copy(q).wait()
        h1_copy(q).wait_send()
        h2_copy(q).wait_send()
        sibling_copy(q).wait_send()
        across_copy(q).wait_send()
        for j in range(1, zs):
            level_copy(q, j).wait_send()
            error_level(q, j).wait_send()
        error_across(q, y).wait_send()
        error_sibling(q, core).wait_send()
    for j in range(1, n):
        swap_copy(j).wait_send()
    for j in range(1, 4):
        feature_copy(0, j).wait_send()
    for j in range(4):
        feature_copy(1, j).wait_send()


def fused_shards(images, keep_index, teacher_weight, student_weight):
    n = lax.axis_size("fsdp")
    patches, width = images.shape[1:]
    keep = keep_index.shape[1]
    depth, columns = teacher_weight.shape
    zs, blocks, part = n // 4, columns // LANE_BLOCK, keep // 2
    pick = (keep_index[0][:, None] == jnp.arange(patches)[None, :]).astype(jnp.bfloat16)
    bf, fl = jnp.bfloat16, jnp.float32
    dma = pltpu.SemaphoreType.DMA
    vm = pltpu.VMEM
    scratch = [
        vm((patches, width), bf), vm((depth, columns), fl), vm((depth, columns), fl),
        vm((depth, columns), fl), vm((depth, columns), fl),
        vm((patches, 128), fl), vm((patches, 128), fl),
        vm((2, 2, zs // 2, patches, depth), bf),
        vm((2, 2, zs, patches, depth), bf),
        vm((blocks, zs, depth, LANE_BLOCK), bf),
        vm((blocks, depth, LANE_BLOCK), bf),
        vm((blocks, 2, patches, LANE_BLOCK), fl),
        vm((blocks, 2, patches, LANE_BLOCK), fl),
        vm((blocks, 2, patches, LANE_BLOCK), fl),
        vm((blocks, patches, LANE_BLOCK), bf),
        vm((blocks, patches, LANE_BLOCK), bf),
        vm((n, part, depth), bf),
        vm((n // 2, part, depth), bf),
        vm((2, 2, 2, zs, part, depth), bf),
        vm((2, depth, n * part), bf),
        vm((blocks, 2, 2, zs, part, LANE_BLOCK), fl),
        vm((blocks, 2, 2, zs, part, LANE_BLOCK), bf),
        vm((blocks, 2, 2, zs, part, LANE_BLOCK), bf),
        vm((blocks, 2, zs, part, LANE_BLOCK), bf),
        vm((blocks, 2, zs, part, LANE_BLOCK), bf),
        vm((blocks, zs, 2, part, LANE_BLOCK), bf),
        vm((blocks, zs - 1, 2, part, LANE_BLOCK), bf),
        vm((blocks, 2, 2, zs, keep, LANE_BLOCK), bf),
        dma((1,)), dma((1,)),
        dma((2, 4)), dma((2, 4)),
        dma((2, blocks, zs - 1)), dma((2, blocks, zs - 1)),
        dma((1,)), dma((1,)),
        dma((n - 1,)), dma((n - 1,)),
        dma((1,)), dma((1,)),
        dma((blocks,)), dma((blocks,)), dma((blocks,)), dma((blocks,)),
        dma((blocks, zs - 1)), dma((blocks, zs - 1)),
        dma((blocks,)), dma((blocks,)), dma((blocks,)), dma((blocks,)),
        dma((blocks, zs - 1)), dma((blocks, zs - 1)),
        dma((blocks,)), dma((blocks,)), dma((blocks,)), dma((blocks,)),
        dma((3,)), dma((blocks + 1,)),
    ]
    out = jax.ShapeDtypeStruct((depth, columns), fl)
    return pl.pallas_call(
        functools.partial(fused, n, keep * n),
        out_shape=(out, out),
        in_specs=[pl.BlockSpec(memory_space=pltpu.VMEM)] + [pl.BlockSpec(memory_space=pl.ANY)] * 3,
        out_specs=(pl.BlockSpec(memory_space=pl.ANY),) * 2,
        scratch_shapes=scratch,
        compiler_params=pltpu.CompilerParams(
            collective_id=0, has_side_effects=True, vmem_limit_bytes=60 * 2**20),
        cost_estimate=pl.CostEstimate(
            flops=2 * n * depth * columns * (patches + 2 * keep), bytes_accessed=2**24, transcendentals=0),
    )(pick, images[0], teacher_weight, student_weight)


def solution(mesh):
    placed = (P("fsdp", None, "tp"), P("fsdp", None), P("fsdp", "tp"), P("fsdp", "tp"))
    fits = mesh.shape["tp"] == 2 and mesh.shape["fsdp"] == 16
    return jax.shard_map(
        fused_shards if fits else shards,
        mesh=mesh,
        in_specs=placed,
        out_specs=(P("fsdp", "tp"), P("fsdp", "tp")),
        check_vma=False,
    )
```

```python
import functools
import math

import jax
import jax.numpy as jnp
from jax import lax
from jax.experimental import pallas as pl
from jax.experimental.pallas import tpu as pltpu
from jax.sharding import PartitionSpec as P

D = 6144


def layer_norm(values):
    floats = values.astype(jnp.float32)
    centre = jnp.mean(floats, axis=-1, keepdims=True)
    centred = floats - centre
    spread = jnp.mean(centred * centred, axis=-1, keepdims=True)
    return (centred * lax.rsqrt(spread + 1e-06)).astype(jnp.bfloat16)


def pick_rows(table, index):
    return jax.vmap(lambda block, rows: block[rows])(table, index)


def row_product(features, piece):
    return jnp.dot(features, piece, preferred_element_type=jnp.float32)


def whole_features(images):
    if lax.axis_size("tp") != 2:
        return lax.all_gather(images, "tp", axis=2, tiled=True)
    other = lax.ppermute(images, "tp", [(0, 1), (1, 0)])
    first = lax.axis_index("tp") == 0
    return jnp.concatenate(
        [jnp.where(first, images, other), jnp.where(first, other, images)], axis=2
    )


def shards(images, keep_index, teacher_weight, student_weight):
    img_count = images.shape[0]
    patch_count = images.shape[1]
    keep_count = keep_index.shape[1]
    columns_dev = teacher_weight.shape[1]
    teacher_next = 0.999 * teacher_weight + (1.0 - 0.999) * student_weight
    teacher_panel = teacher_next.astype(jnp.bfloat16)
    student_panel = student_weight.astype(jnp.bfloat16)
    whole_panel = lax.all_gather(teacher_panel, "fsdp", axis=0, tiled=True)
    normed = layer_norm(whole_features(images))
    flat_all = normed.reshape(img_count * patch_count, D)
    picked = pick_rows(normed, keep_index).reshape(img_count * keep_count, D)
    owned = lax.all_to_all(picked, "fsdp", split_axis=1, concat_axis=0, tiled=True)
    partial = row_product(owned, student_panel).astype(jnp.bfloat16)
    student_out = lax.psum_scatter(partial, "fsdp", scatter_dimension=0, tiled=True)
    student_out = student_out.astype(jnp.float32)
    teacher_out = row_product(flat_all, whole_panel)
    teacher_out = teacher_out.reshape(img_count, patch_count, columns_dev)
    centre = jnp.mean(teacher_out, axis=1, keepdims=True)
    centred_out = teacher_out - centre
    spread = jnp.mean(centred_out * centred_out, axis=1, keepdims=True)
    target = centred_out * lax.rsqrt(spread + 1e-05)
    target_kept = pick_rows(target, keep_index).reshape(img_count * keep_count, columns_dev)
    total_kept = img_count * keep_count * lax.axis_size("fsdp")
    error = ((student_out - target_kept) * (1.0 / math.sqrt(total_kept))).astype(jnp.bfloat16)
    student_grad = lax.dot_general(
        owned,
        lax.all_gather(error, "fsdp", axis=0, tiled=True),
        (((0,), (0,)), ((), ())),
        preferred_element_type=jnp.float32,
    )
    return (teacher_next, student_grad)


MESH = pl.DeviceIdType.MESH
LANE_BLOCK = 256


def fused(n, total_kept, index, images_hbm, tw_hbm, sw_hbm, tnext_hbm, grad_hbm, pick, images, tw, sw, tnext, grad, stat, stat_in, nbuf, xk, wt, ws,
          pt, os_, or_, ys_, yr_, pb, pxs, owned, turned, pf, h1s, h1r, h2s, h2r, h3s, h3r, ebuf,
          sts, str_, xs, xr, ls, lr, ps, pr, as_, ar, ss, sr, h1ss, h1rs, h2ss, h2rs, h3ss, h3rs,
          oss, ors, yss, yrs, zss, zrs, ess, ers, bss, brs, loads, stores):
    f = lax.axis_index("fsdp")
    t = lax.axis_index("tp")
    zs = n // 4
    side = n // 2
    z = lax.div(f, 4)
    spot = lax.rem(f, 4)
    y = lax.div(spot, 2)
    core = lax.rem(spot, 2)
    other = 1 - core
    patches, width = images.shape
    depth = tw.shape[0]
    blocks = tw.shape[1] // LANE_BLOCK
    keep = index.shape[1]
    part = keep // 2
    sibling = (4 * z + 2 * y + other, t)
    across = (4 * z + 2 * (1 - y) + core, t)
    mirror = (f, 1 - t)

    def remote(src, dst, send, recv, device):
        return pltpu.make_async_remote_copy(
            src_ref=src, dst_ref=dst, send_sem=send, recv_sem=recv,
            device_id=device, device_id_type=MESH)

    fetched = [pltpu.make_async_copy(a, b, loads.at[i])
               for i, (a, b) in enumerate(((tw_hbm, tw), (sw_hbm, sw), (images_hbm, images)))]
    for copy in fetched:
        copy.start()

    barrier = pltpu.get_barrier_semaphore()
    for j in range(1, n):
        pl.semaphore_signal(barrier, inc=1, device_id=(lax.rem(f + j, n), t), device_id_type=MESH)
    for j in range(4):
        pl.semaphore_signal(
            barrier, inc=1, device_id=(4 * z + lax.rem(spot + j, 4), 1 - t), device_id_type=MESH)
    chosen = lax.broadcasted_iota(jnp.int32, (patches, keep), 0) == index[...]
    pick[...] = jnp.where(chosen, 1.0, 0.0).T.astype(jnp.bfloat16)
    pl.semaphore_wait(barrier, n + 3)

    def line_copy(way, q, i, source, to):
        ref = wt.at[q, source]
        return remote(ref, ref, ls.at[way, q, i], lr.at[way, q, i], to)

    down = (f - 4, t)
    up = (f + 4, t)
    tile = 64
    fetched[0].wait()
    fetched[1].wait()
    for q in range(blocks):
        columns = slice(q * LANE_BLOCK, (q + 1) * LANE_BLOCK)

        @pl.loop(0, depth // tile)
        def _(i):
            rows = pl.ds(pl.multiple_of(i * tile, tile), tile)
            student = sw[rows, columns]
            following = 0.999 * tw[rows, columns] + (1.0 - 0.999) * student
            tnext[rows, columns] = following
            wt[q, z, rows, :] = following.astype(jnp.bfloat16)
            ws[q, rows, :] = student.astype(jnp.bfloat16)

        @pl.when(z > 0)
        def _():
            line_copy(0, q, 0, z, down).start()

        @pl.when(z < zs - 1)
        def _():
            line_copy(1, q, 0, z, up).start()

    next_out = pltpu.make_async_copy(tnext, tnext_hbm, stores.at[blocks])
    next_out.start()

    fetched[2].wait()
    lane = lax.broadcasted_iota(jnp.int32, (16, 128), 1)

    @pl.loop(0, patches // 16)
    def _(i):
        rows = pl.ds(pl.multiple_of(i * 16, 16), 16)
        values = images[rows, :].astype(jnp.float32)
        centre = jnp.sum(values, axis=1, keepdims=True) * (1.0 / width)
        values = values - centre
        spread = jnp.sum(values * values, axis=1, keepdims=True)
        stat[rows, :] = jnp.where(lane < 64, centre, spread)

    stats = remote(stat, stat_in, sts.at[0], str_.at[0], mirror)
    stats.start()

    def pump(i, q):
        @pl.when(z + 1 + i < zs)
        def _():
            line_copy(0, q, i, z + 1 + i, sibling).wait_recv()
            if i < zs - 2:
                @pl.when(z > 0)
                def _():
                    line_copy(0, q, i + 1, z + 1 + i, down).start()

        @pl.when(z - 1 - i >= 0)
        def _():
            line_copy(1, q, i, z - 1 - i, sibling).wait_recv()
            if i < zs - 2:
                @pl.when(z < zs - 1)
                def _():
                    line_copy(1, q, i + 1, z - 1 - i, up).start()

    stats.wait_recv()

    @pl.loop(0, patches // 16)
    def _(i):
        rows = pl.ds(pl.multiple_of(i * 16, 16), 16)
        here, there = stat[rows, :], stat_in[rows, :]
        centre = (here[:, 0:1] + there[:, 0:1]) * 0.5
        apart = here[:, 0:1] - there[:, 0:1]
        spread = (here[:, 64:65] + there[:, 64:65]) * (0.5 / width) + apart * apart * 0.25
        scaled = ((images[rows, :].astype(jnp.float32) - centre) * lax.rsqrt(spread + 1e-06)).astype(jnp.bfloat16)
        for j in range(side):
            nbuf[j % 4 // 2, j % 2, j // 4, rows, :] = scaled[:, j * depth:(j + 1) * depth]

    @pl.loop(0, side // 4)
    def _(level):
        for j in range(4):
            rows = jnp.dot(pick[...], nbuf[j // 2, j % 2, level],
                           preferred_element_type=jnp.float32).astype(jnp.bfloat16)
            pb[side * t + 4 * level + j] = rows[:part]
            pxs[4 * level + j] = rows[part:]

    kept_out = remote(pxs, pb.at[pl.ds(side * t, side)], ps.at[0], pr.at[0], mirror)
    kept_out.start()

    def feature_copy(plane, j):
        to = lax.rem(spot + j, 4)
        return remote(nbuf.at[lax.div(to, 2), lax.rem(to, 2)], xk.at[y, core, pl.ds(2 * t, 2)],
                      xs.at[plane, j], xr.at[plane, j],
                      (4 * z + to, t if plane == 0 else 1 - t))

    xk[y, core, pl.ds(2 * t, 2)] = nbuf[y, core]
    kept_in = remote(pxs, pb.at[pl.ds(side * (1 - t), side)], ps.at[0], pr.at[0], mirror)
    kept_in.wait_recv()

    def half_of(device):
        return lax.rem(t + lax.div(device, side), 2)

    def swap_copy(j):
        to = lax.rem(f + j, n)
        return remote(pb.at[to], owned.at[half_of(to), core, y, z], as_.at[j - 1], ar.at[j - 1], (to, t))

    mine = half_of(f)
    for j in range(1, n):
        swap_copy(j).start()
    owned[mine, core, y, z] = pb[f]
    for j in range(1, 4):
        feature_copy(0, j).start()
    for j in range(2):
        feature_copy(1, j).start()

    for q in range(blocks // 2):
        pump(0, q)

    for j in range(1, n):
        origin = lax.rem(f + n - j, n)
        remote(pb.at[0],
               owned.at[mine, lax.rem(origin, 2), lax.div(lax.rem(origin, 4), 2), lax.div(origin, 4)],
               as_.at[j - 1], ar.at[j - 1], (origin, t)).wait_recv()
    halves = remote(owned.at[mine], owned.at[mine], ss.at[0], sr.at[0], mirror)
    halves.start()
    for j in range(2, 4):
        feature_copy(1, j).start()
    for q in range(blocks // 2, blocks):
        pump(0, q)
    remote(owned.at[1 - mine], owned.at[1 - mine], ss.at[0], sr.at[0], mirror).wait_recv()

    split = (2, 2, zs, part, LANE_BLOCK)
    rows_core = 4 * zs * part

    def h1_copy(q):
        return remote(h1s.at[q], h1r.at[q], h1ss.at[q], h1rs.at[q], sibling)

    def h2_copy(q):
        return remote(h2s.at[q], h2r.at[q], h2ss.at[q], h2rs.at[q], across)

    def chain_copy(way, q, e, to):
        return remote(h3s.at[way, q, e], h3r.at[way, q, e], h3ss.at[way, q, e], h3rs.at[way, q, e], to)

    def chain(q, way, first):
        for e in range(zs):
            ahead = e < z if way == 0 else e > z

            @pl.when(ahead)
            def _():
                value = pf[q, :, y, e]
                if not first:
                    chain_copy(way, q, e, sibling).wait_recv()
                    value = value + h3r[way, q, e].astype(jnp.float32)
                h3s[way, q, e] = value.astype(jnp.bfloat16)
                chain_copy(way, q, e, down if way == 0 else up).start()

    def chain_step(q, hop):
        if hop == 0:
            @pl.when(z == zs - 1)
            def _():
                chain(q, 0, True)

            @pl.when(z == 0)
            def _():
                chain(q, 1, True)
        else:
            @pl.when(z == zs - 1 - hop)
            def _():
                chain(q, 0, False)

            @pl.when(z == hop)
            def _():
                chain(q, 1, False)

    @pl.loop(0, blocks)
    def _(q):
        panel = ws[q]
        send = jnp.dot(owned[:, other].reshape(rows_core, depth), panel,
                       preferred_element_type=jnp.float32)
        h1s[q] = send.astype(jnp.bfloat16).reshape(split)
        h1_copy(q).start()
        own = jnp.dot(owned[:, core].reshape(rows_core, depth), panel,
                      preferred_element_type=jnp.float32)
        pf[q] = own.reshape(split)

    @pl.loop(0, blocks)
    def _(q):
        h1_copy(q).wait_recv()
        for g in range(2):
            h2s[q, g] = (pf[q, g, 1 - y] + h1r[q, g, 1 - y].astype(jnp.float32)).astype(jnp.bfloat16)
            pf[q, g, y] += h1r[q, g, y].astype(jnp.float32)
        h2_copy(q).start()

    for g in range(2):
        turned[g] = owned[g].reshape(rows_core, depth).T

    for q in range(blocks):
        pump(1, q)
        h2_copy(q).wait_recv()

        @pl.loop(0, zs)
        def _(level):
            for g in range(2):
                pf[q, g, y, level] += h2r[q, g, level].astype(jnp.float32)

        chain_step(q, 0)
        for hop in range(1, zs - 1):
            if q >= hop:
                chain_step(q - hop, hop)
    for late in range(1, zs - 1):
        for hop in range(late, zs - 1):
            chain_step(blocks - 1 + late - hop, hop)

    def feature_wait(plane, j):
        origin = lax.rem(spot + 4 - j, 4)
        first = 2 * t if plane == 0 else 2 * (1 - t)
        remote(nbuf.at[0, 0], xk.at[lax.div(origin, 2), lax.rem(origin, 2), pl.ds(first, 2)],
               xs.at[plane, j], xr.at[plane, j], sibling).wait_recv()

    for j in range(1, 4):
        feature_wait(0, j)
    for j in range(4):
        feature_wait(1, j)

    def sibling_copy(q):
        return remote(os_.at[q], or_.at[q], oss.at[q], ors.at[q], sibling)

    def across_copy(q):
        return remote(ys_.at[q], yr_.at[q], yss.at[q], yrs.at[q], across)

    def error_level(q, j):
        ref = ebuf.at[q, core, y, z]
        return remote(ref, ref, zss.at[q, j - 1], zrs.at[q, j - 1], (4 * lax.rem(z + j, zs) + spot, t))

    def error_across(q, row):
        ref = ebuf.at[q, core, row]
        return remote(ref, ref, ess.at[q], ers.at[q], across)

    def error_sibling(q, owner):
        ref = ebuf.at[q, owner]
        return remote(ref, ref, bss.at[q], brs.at[q], sibling)

    def product(q):
        if zs > 2:
            pump(zs - 2, q)

        @pl.loop(0, 2)
        def _(row):
            for target, owner in ((os_, other), (pt, core)):
                total = jnp.dot(xk[row, owner, 0], wt[q, 0], preferred_element_type=jnp.float32)
                for level in range(1, zs):
                    total += jnp.dot(xk[row, owner, level], wt[q, level],
                                     preferred_element_type=jnp.float32)
                target[q, row] = total

        sibling_copy(q).start()

    def cores_add(q):
        sibling_copy(q).wait_recv()
        ys_[q] = (pt[q, 1 - y] + or_[q, 1 - y]).astype(jnp.bfloat16)
        across_copy(q).start()
        pt[q, y] += or_[q, y]

    def error_of(q):
        for way in range(2):
            @pl.when(z < zs - 1 if way == 0 else z > 0)
            def _():
                chain_copy(way, q, z, sibling).wait_recv()
                pf[q, :, y, z] += h3r[way, q, z].astype(jnp.float32)
        across_copy(q).wait_recv()
        value = pt[q, y] + yr_[q].astype(jnp.float32)
        centre = jnp.sum(value, axis=0, keepdims=True) * (1.0 / patches)
        value = value - centre
        spread = jnp.sum(value * value, axis=0, keepdims=True) * (1.0 / patches)
        target = value * lax.rsqrt(spread + 1e-05)
        upper = target.astype(jnp.bfloat16)
        lower = (target - upper.astype(jnp.float32)).astype(jnp.bfloat16)
        kept = (jnp.dot(pick[...], upper, preferred_element_type=jnp.float32)
                + jnp.dot(pick[...], lower, preferred_element_type=jnp.float32))
        student = pf[q, :, y, z]
        student = student.reshape(keep, LANE_BLOCK)
        ebuf[q, core, y, z] = ((student - kept) * (1.0 / math.sqrt(total_kept))).astype(jnp.bfloat16)
        for j in range(1, zs):
            error_level(q, j).start()

    def levels_in(q):
        for j in range(1, zs):
            ref = ebuf.at[q, core, y, lax.rem(z + zs - j, zs)]
            remote(ref, ref, zss.at[q, j - 1], zrs.at[q, j - 1], sibling).wait_recv()
        error_across(q, y).start()

    def across_in(q):
        error_across(q, 1 - y).wait_recv()
        error_sibling(q, core).start()

    def finish(q):
        error_sibling(q, other).wait_recv()
        total = None
        for g in range(2):
            errors = ebuf[q, :, :, :, g * part:(g + 1) * part].reshape(rows_core, LANE_BLOCK)
            term = jnp.dot(turned[g], errors, preferred_element_type=jnp.float32)
            total = term if total is None else total + term
        grad[:, q * LANE_BLOCK:(q + 1) * LANE_BLOCK] = total
        grad_copy(q).start()

    def grad_copy(q):
        columns = pl.ds(q * LANE_BLOCK, LANE_BLOCK)
        return pltpu.make_async_copy(grad.at[:, columns], grad_hbm.at[:, columns], stores.at[q])

    stages = ((product, 0), (error_of, 1), (cores_add, 0), (levels_in, 2), (across_in, 3), (finish, 4))
    for wave in range(blocks + 4):
        for stage, lag in stages:
            if 0 <= wave - lag < blocks:
                stage(wave - lag)

    for copy in (stats, kept_out, halves):
        copy.wait_send()
    next_out.wait()
    for q in range(blocks):
        for i in range(zs - 1):
            @pl.when((z > 0) & (z + i < zs))
            def _():
                line_copy(0, q, i, z, sibling).wait_send()

            @pl.when((z < zs - 1) & (z - i >= 0))
            def _():
                line_copy(1, q, i, z, sibling).wait_send()
        grad_copy(q).wait()
        h1_copy(q).wait_send()
        h2_copy(q).wait_send()
        sibling_copy(q).wait_send()
        across_copy(q).wait_send()
        for j in range(1, zs):
            error_level(q, j).wait_send()
        error_across(q, y).wait_send()
        error_sibling(q, core).wait_send()
        for e in range(zs):
            for way in range(2):
                @pl.when(e < z if way == 0 else e > z)
                def _():
                    chain_copy(way, q, e, sibling).wait_send()
    for j in range(1, n):
        swap_copy(j).wait_send()
    for j in range(1, 4):
        feature_copy(0, j).wait_send()
    for j in range(4):
        feature_copy(1, j).wait_send()


def fused_shards(images, keep_index, teacher_weight, student_weight):
    n = lax.axis_size("fsdp")
    patches, width = images.shape[1:]
    keep = keep_index.shape[1]
    depth, columns = teacher_weight.shape
    zs, blocks, part = n // 4, columns // LANE_BLOCK, keep // 2
    bf, fl = jnp.bfloat16, jnp.float32
    dma = pltpu.SemaphoreType.DMA
    vm = pltpu.VMEM
    scratch = [
        vm((keep, patches), bf),
        vm((patches, width), bf), vm((depth, columns), fl), vm((depth, columns), fl),
        vm((depth, columns), fl), vm((depth, columns), fl),
        vm((patches, 128), fl), vm((patches, 128), fl),
        vm((2, 2, zs // 2, patches, depth), bf),
        vm((2, 2, zs, patches, depth), bf),
        vm((blocks, zs, depth, LANE_BLOCK), bf),
        vm((blocks, depth, LANE_BLOCK), bf),
        vm((blocks, 2, patches, LANE_BLOCK), fl),
        vm((blocks, 2, patches, LANE_BLOCK), fl),
        vm((blocks, 2, patches, LANE_BLOCK), fl),
        vm((blocks, patches, LANE_BLOCK), bf),
        vm((blocks, patches, LANE_BLOCK), bf),
        vm((n, part, depth), bf),
        vm((n // 2, part, depth), bf),
        vm((2, 2, 2, zs, part, depth), bf),
        vm((2, depth, n * part), bf),
        vm((blocks, 2, 2, zs, part, LANE_BLOCK), fl),
        vm((blocks, 2, 2, zs, part, LANE_BLOCK), bf),
        vm((blocks, 2, 2, zs, part, LANE_BLOCK), bf),
        vm((blocks, 2, zs, part, LANE_BLOCK), bf),
        vm((blocks, 2, zs, part, LANE_BLOCK), bf),
        vm((2, blocks, zs, 2, part, LANE_BLOCK), bf),
        vm((2, blocks, zs, 2, part, LANE_BLOCK), bf),
        vm((blocks, 2, 2, zs, keep, LANE_BLOCK), bf),
        dma((1,)), dma((1,)),
        dma((2, 4)), dma((2, 4)),
        dma((2, blocks, zs - 1)), dma((2, blocks, zs - 1)),
        dma((1,)), dma((1,)),
        dma((n - 1,)), dma((n - 1,)),
        dma((1,)), dma((1,)),
        dma((blocks,)), dma((blocks,)), dma((blocks,)), dma((blocks,)),
        dma((2, blocks, zs)), dma((2, blocks, zs)),
        dma((blocks,)), dma((blocks,)), dma((blocks,)), dma((blocks,)),
        dma((blocks, zs - 1)), dma((blocks, zs - 1)),
        dma((blocks,)), dma((blocks,)), dma((blocks,)), dma((blocks,)),
        dma((3,)), dma((blocks + 1,)),
    ]
    out = jax.ShapeDtypeStruct((depth, columns), fl)
    return pl.pallas_call(
        functools.partial(fused, n, keep * n),
        out_shape=(out, out),
        in_specs=[pl.BlockSpec(memory_space=pltpu.VMEM)] + [pl.BlockSpec(memory_space=pl.ANY)] * 3,
        out_specs=(pl.BlockSpec(memory_space=pl.ANY),) * 2,
        scratch_shapes=scratch,
        compiler_params=pltpu.CompilerParams(
            collective_id=0, has_side_effects=True, vmem_limit_bytes=60 * 2**20),
        cost_estimate=pl.CostEstimate(
            flops=2 * n * depth * columns * (patches + 2 * keep), bytes_accessed=2**24, transcendentals=0),
    )(keep_index, images[0], teacher_weight, student_weight)


def solution(mesh):
    placed = (P("fsdp", None, "tp"), P("fsdp", None), P("fsdp", "tp"), P("fsdp", "tp"))
    fits = mesh.shape["tp"] == 2 and mesh.shape["fsdp"] == 16
    return jax.shard_map(
        fused_shards if fits else shards,
        mesh=mesh,
        in_specs=placed,
        out_specs=(P("fsdp", "tp"), P("fsdp", "tp")),
        check_vma=False,
    )
```

```python
import functools
import math

import jax
import jax.numpy as jnp
from jax import lax
from jax.experimental import pallas as pl
from jax.experimental.pallas import tpu as pltpu
from jax.sharding import PartitionSpec as P

D = 6144


def layer_norm(values):
    floats = values.astype(jnp.float32)
    centre = jnp.mean(floats, axis=-1, keepdims=True)
    centred = floats - centre
    spread = jnp.mean(centred * centred, axis=-1, keepdims=True)
    return (centred * lax.rsqrt(spread + 1e-06)).astype(jnp.bfloat16)


def pick_rows(table, index):
    return jax.vmap(lambda block, rows: block[rows])(table, index)


def row_product(features, piece):
    return jnp.dot(features, piece, preferred_element_type=jnp.float32)


def whole_features(images):
    if lax.axis_size("tp") != 2:
        return lax.all_gather(images, "tp", axis=2, tiled=True)
    other = lax.ppermute(images, "tp", [(0, 1), (1, 0)])
    first = lax.axis_index("tp") == 0
    return jnp.concatenate(
        [jnp.where(first, images, other), jnp.where(first, other, images)], axis=2
    )


def shards(images, keep_index, teacher_weight, student_weight):
    img_count = images.shape[0]
    patch_count = images.shape[1]
    keep_count = keep_index.shape[1]
    columns_dev = teacher_weight.shape[1]
    teacher_next = 0.999 * teacher_weight + (1.0 - 0.999) * student_weight
    teacher_panel = teacher_next.astype(jnp.bfloat16)
    student_panel = student_weight.astype(jnp.bfloat16)
    whole_panel = lax.all_gather(teacher_panel, "fsdp", axis=0, tiled=True)
    normed = layer_norm(whole_features(images))
    flat_all = normed.reshape(img_count * patch_count, D)
    picked = pick_rows(normed, keep_index).reshape(img_count * keep_count, D)
    owned = lax.all_to_all(picked, "fsdp", split_axis=1, concat_axis=0, tiled=True)
    partial = row_product(owned, student_panel).astype(jnp.bfloat16)
    student_out = lax.psum_scatter(partial, "fsdp", scatter_dimension=0, tiled=True)
    student_out = student_out.astype(jnp.float32)
    teacher_out = row_product(flat_all, whole_panel)
    teacher_out = teacher_out.reshape(img_count, patch_count, columns_dev)
    centre = jnp.mean(teacher_out, axis=1, keepdims=True)
    centred_out = teacher_out - centre
    spread = jnp.mean(centred_out * centred_out, axis=1, keepdims=True)
    target = centred_out * lax.rsqrt(spread + 1e-05)
    target_kept = pick_rows(target, keep_index).reshape(img_count * keep_count, columns_dev)
    total_kept = img_count * keep_count * lax.axis_size("fsdp")
    error = ((student_out - target_kept) * (1.0 / math.sqrt(total_kept))).astype(jnp.bfloat16)
    student_grad = lax.dot_general(
        owned,
        lax.all_gather(error, "fsdp", axis=0, tiled=True),
        (((0,), (0,)), ((), ())),
        preferred_element_type=jnp.float32,
    )
    return (teacher_next, student_grad)


MESH = pl.DeviceIdType.MESH
LANE_BLOCK = 256


def fused(n, total_kept, index, images_hbm, tw_hbm, sw_hbm, tnext_hbm, grad_hbm, pick, images, tw, sw, tnext, grad, stat, stat_in, nbuf, xk, wt, ws,
          pt, os_, or_, ys_, yr_, pb, pxs, owned, turned, pf, h1s, h1r, h2s, h2r, h3s, h3r, ebuf,
          sts, str_, xs, xr, ls, lr, ps, pr, as_, ar, ss, sr, h1ss, h1rs, h2ss, h2rs, h3ss, h3rs,
          oss, ors, yss, yrs, zss, zrs, ess, ers, bss, brs, loads, stores):
    f = lax.axis_index("fsdp")
    t = lax.axis_index("tp")
    zs = n // 4
    side = n // 2
    z = lax.div(f, 4)
    spot = lax.rem(f, 4)
    y = lax.div(spot, 2)
    core = lax.rem(spot, 2)
    other = 1 - core
    patches, width = images.shape
    depth = tw.shape[0]
    blocks = tw.shape[1] // LANE_BLOCK
    keep = index.shape[1]
    part = keep // 2
    sibling = (4 * z + 2 * y + other, t)
    across = (4 * z + 2 * (1 - y) + core, t)
    mirror = (f, 1 - t)

    def remote(src, dst, send, recv, device):
        return pltpu.make_async_remote_copy(
            src_ref=src, dst_ref=dst, send_sem=send, recv_sem=recv,
            device_id=device, device_id_type=MESH)

    fetched = [pltpu.make_async_copy(a, b, loads.at[i])
               for i, (a, b) in enumerate(((tw_hbm, tw), (sw_hbm, sw), (images_hbm, images)))]
    for copy in fetched:
        copy.start()

    barrier = pltpu.get_barrier_semaphore()
    for j in range(1, n):
        pl.semaphore_signal(barrier, inc=1, device_id=(lax.rem(f + j, n), t), device_id_type=MESH)
    for j in range(4):
        pl.semaphore_signal(
            barrier, inc=1, device_id=(4 * z + lax.rem(spot + j, 4), 1 - t), device_id_type=MESH)
    chosen = lax.broadcasted_iota(jnp.int32, (patches, keep), 0) == index[...]
    pick[...] = jnp.where(chosen, 1.0, 0.0).T.astype(jnp.bfloat16)
    pl.semaphore_wait(barrier, n + 3)

    def line_copy(way, q, i, source, to):
        ref = wt.at[q, source]
        return remote(ref, ref, ls.at[way, q, i], lr.at[way, q, i], to)

    down = (f - 4, t)
    up = (f + 4, t)
    tile = 64
    fetched[0].wait()
    fetched[1].wait()
    for q in range(blocks):
        columns = slice(q * LANE_BLOCK, (q + 1) * LANE_BLOCK)

        @pl.loop(0, depth // tile)
        def _(i):
            rows = pl.ds(pl.multiple_of(i * tile, tile), tile)
            student = sw[rows, columns]
            following = 0.999 * tw[rows, columns] + (1.0 - 0.999) * student
            tnext[rows, columns] = following
            wt[q, z, rows, :] = following.astype(jnp.bfloat16)
            ws[q, rows, :] = student.astype(jnp.bfloat16)

        @pl.when(z > 0)
        def _():
            line_copy(0, q, 0, z, down).start()

        @pl.when(z < zs - 1)
        def _():
            line_copy(1, q, 0, z, up).start()

    next_out = pltpu.make_async_copy(tnext, tnext_hbm, stores.at[blocks])
    next_out.start()

    fetched[2].wait()
    lane = lax.broadcasted_iota(jnp.int32, (16, 128), 1)

    @pl.loop(0, patches // 16)
    def _(i):
        rows = pl.ds(pl.multiple_of(i * 16, 16), 16)
        values = images[rows, :].astype(jnp.float32)
        centre = jnp.sum(values, axis=1, keepdims=True) * (1.0 / width)
        values = values - centre
        spread = jnp.sum(values * values, axis=1, keepdims=True)
        stat[rows, :] = jnp.where(lane < 64, centre, spread)

    stats = remote(stat, stat_in, sts.at[0], str_.at[0], mirror)
    stats.start()

    def pump(i, q):
        @pl.when(z + 1 + i < zs)
        def _():
            line_copy(0, q, i, z + 1 + i, sibling).wait_recv()
            if i < zs - 2:
                @pl.when(z > 0)
                def _():
                    line_copy(0, q, i + 1, z + 1 + i, down).start()

        @pl.when(z - 1 - i >= 0)
        def _():
            line_copy(1, q, i, z - 1 - i, sibling).wait_recv()
            if i < zs - 2:
                @pl.when(z < zs - 1)
                def _():
                    line_copy(1, q, i + 1, z - 1 - i, up).start()

    stats.wait_recv()

    @pl.loop(0, patches // 16)
    def _(i):
        rows = pl.ds(pl.multiple_of(i * 16, 16), 16)
        here, there = stat[rows, :], stat_in[rows, :]
        centre = (here[:, 0:1] + there[:, 0:1]) * 0.5
        apart = here[:, 0:1] - there[:, 0:1]
        spread = (here[:, 64:65] + there[:, 64:65]) * (0.5 / width) + apart * apart * 0.25
        scaled = ((images[rows, :].astype(jnp.float32) - centre) * lax.rsqrt(spread + 1e-06)).astype(jnp.bfloat16)
        for j in range(side):
            nbuf[j % 4 // 2, j % 2, j // 4, rows, :] = scaled[:, j * depth:(j + 1) * depth]

    @pl.loop(0, side // 4)
    def _(level):
        for j in range(4):
            rows = jnp.dot(pick[...], nbuf[j // 2, j % 2, level],
                           preferred_element_type=jnp.float32).astype(jnp.bfloat16)
            pb[side * t + 4 * level + j] = rows[:part]
            pxs[4 * level + j] = rows[part:]

    kept_out = remote(pxs, pb.at[pl.ds(side * t, side)], ps.at[0], pr.at[0], mirror)
    kept_out.start()

    def feature_copy(plane, j):
        to = lax.rem(spot + j, 4)
        return remote(nbuf.at[lax.div(to, 2), lax.rem(to, 2)], xk.at[y, core, pl.ds(2 * t, 2)],
                      xs.at[plane, j], xr.at[plane, j],
                      (4 * z + to, t if plane == 0 else 1 - t))

    xk[y, core, pl.ds(2 * t, 2)] = nbuf[y, core]
    kept_in = remote(pxs, pb.at[pl.ds(side * (1 - t), side)], ps.at[0], pr.at[0], mirror)
    kept_in.wait_recv()

    def half_of(device):
        return lax.rem(t + lax.div(device, side), 2)

    def swap_copy(j):
        to = lax.rem(f + j, n)
        return remote(pb.at[to], owned.at[half_of(to), core, y, z], as_.at[j - 1], ar.at[j - 1], (to, t))

    mine = half_of(f)
    for j in range(1, n):
        swap_copy(j).start()
    owned[mine, core, y, z] = pb[f]
    for j in range(1, 4):
        feature_copy(0, j).start()
    for j in range(2):
        feature_copy(1, j).start()

    for q in range(blocks // 2):
        pump(0, q)

    for j in range(1, n):
        origin = lax.rem(f + n - j, n)
        remote(pb.at[0],
               owned.at[mine, lax.rem(origin, 2), lax.div(lax.rem(origin, 4), 2), lax.div(origin, 4)],
               as_.at[j - 1], ar.at[j - 1], (origin, t)).wait_recv()
    halves = remote(owned.at[mine], owned.at[mine], ss.at[0], sr.at[0], mirror)
    halves.start()
    for j in range(2, 4):
        feature_copy(1, j).start()
    for q in range(blocks // 2, blocks):
        pump(0, q)
    remote(owned.at[1 - mine], owned.at[1 - mine], ss.at[0], sr.at[0], mirror).wait_recv()

    split = (2, 2, zs, part, LANE_BLOCK)
    rows_core = 4 * zs * part

    def h1_copy(q):
        return remote(h1s.at[q], h1r.at[q], h1ss.at[q], h1rs.at[q], sibling)

    def h2_copy(q):
        return remote(h2s.at[q], h2r.at[q], h2ss.at[q], h2rs.at[q], across)

    def chain_copy(way, q, e, to):
        return remote(h3s.at[way, q, e], h3r.at[way, q, e], h3ss.at[way, q, e], h3rs.at[way, q, e], to)

    def chain(q, way, first):
        for e in range(zs):
            ahead = e < z if way == 0 else e > z

            @pl.when(ahead)
            def _():
                value = pf[q, :, y, e]
                if not first:
                    chain_copy(way, q, e, sibling).wait_recv()
                    value = value + h3r[way, q, e].astype(jnp.float32)
                h3s[way, q, e] = value.astype(jnp.bfloat16)
                chain_copy(way, q, e, down if way == 0 else up).start()

    def chain_step(q, hop):
        if hop == 0:
            @pl.when(z == zs - 1)
            def _():
                chain(q, 0, True)

            @pl.when(z == 0)
            def _():
                chain(q, 1, True)
        else:
            @pl.when(z == zs - 1 - hop)
            def _():
                chain(q, 0, False)

            @pl.when(z == hop)
            def _():
                chain(q, 1, False)

    @pl.loop(0, blocks)
    def _(q):
        panel = ws[q]
        send = jnp.dot(owned[:, other].reshape(rows_core, depth), panel,
                       preferred_element_type=jnp.float32)
        h1s[q] = send.astype(jnp.bfloat16).reshape(split)
        h1_copy(q).start()
        own = jnp.dot(owned[:, core].reshape(rows_core, depth), panel,
                      preferred_element_type=jnp.float32)
        pf[q] = own.reshape(split)

    for q in range(blocks // 2):
        pump(1, q)

    @pl.loop(0, blocks)
    def _(q):
        h1_copy(q).wait_recv()
        for g in range(2):
            h2s[q, g] = (pf[q, g, 1 - y] + h1r[q, g, 1 - y].astype(jnp.float32)).astype(jnp.bfloat16)
            pf[q, g, y] += h1r[q, g, y].astype(jnp.float32)
        h2_copy(q).start()

    for g in range(2):
        turned[g] = owned[g].reshape(rows_core, depth).T

    for q in range(blocks):
        if q >= blocks // 2:
            pump(1, q)
        h2_copy(q).wait_recv()

        @pl.loop(0, zs)
        def _(level):
            for g in range(2):
                pf[q, g, y, level] += h2r[q, g, level].astype(jnp.float32)

        chain_step(q, 0)
        for hop in range(1, zs - 1):
            if q >= hop:
                chain_step(q - hop, hop)
    for late in range(1, zs - 1):
        for hop in range(late, zs - 1):
            chain_step(blocks - 1 + late - hop, hop)

    def feature_wait(plane, j):
        origin = lax.rem(spot + 4 - j, 4)
        first = 2 * t if plane == 0 else 2 * (1 - t)
        remote(nbuf.at[0, 0], xk.at[lax.div(origin, 2), lax.rem(origin, 2), pl.ds(first, 2)],
               xs.at[plane, j], xr.at[plane, j], sibling).wait_recv()

    for j in range(1, 4):
        feature_wait(0, j)
    for j in range(4):
        feature_wait(1, j)

    def sibling_copy(q):
        return remote(os_.at[q], or_.at[q], oss.at[q], ors.at[q], sibling)

    def across_copy(q):
        return remote(ys_.at[q], yr_.at[q], yss.at[q], yrs.at[q], across)

    def error_level(q, j):
        ref = ebuf.at[q, core, y, z]
        return remote(ref, ref, zss.at[q, j - 1], zrs.at[q, j - 1], (4 * lax.rem(z + j, zs) + spot, t))

    def error_across(q, row):
        ref = ebuf.at[q, core, row]
        return remote(ref, ref, ess.at[q], ers.at[q], across)

    def error_sibling(q, owner):
        ref = ebuf.at[q, owner]
        return remote(ref, ref, bss.at[q], brs.at[q], sibling)

    def product(q):
        if zs > 2:
            pump(zs - 2, q)

        @pl.loop(0, 2)
        def _(row):
            for target, owner in ((os_, other), (pt, core)):
                total = jnp.dot(xk[row, owner, 0], wt[q, 0], preferred_element_type=jnp.float32)
                for level in range(1, zs):
                    total += jnp.dot(xk[row, owner, level], wt[q, level],
                                     preferred_element_type=jnp.float32)
                target[q, row] = total

        sibling_copy(q).start()

    def cores_add(q):
        sibling_copy(q).wait_recv()
        ys_[q] = (pt[q, 1 - y] + or_[q, 1 - y]).astype(jnp.bfloat16)
        across_copy(q).start()
        pt[q, y] += or_[q, y]

    def error_of(q):
        for way in range(2):
            @pl.when(z < zs - 1 if way == 0 else z > 0)
            def _():
                chain_copy(way, q, z, sibling).wait_recv()
                pf[q, :, y, z] += h3r[way, q, z].astype(jnp.float32)
        across_copy(q).wait_recv()
        value = pt[q, y] + yr_[q].astype(jnp.float32)
        centre = jnp.sum(value, axis=0, keepdims=True) * (1.0 / patches)
        value = value - centre
        spread = jnp.sum(value * value, axis=0, keepdims=True) * (1.0 / patches)
        target = value * lax.rsqrt(spread + 1e-05)
        upper = target.astype(jnp.bfloat16)
        lower = (target - upper.astype(jnp.float32)).astype(jnp.bfloat16)
        kept = (jnp.dot(pick[...], upper, preferred_element_type=jnp.float32)
                + jnp.dot(pick[...], lower, preferred_element_type=jnp.float32))
        student = pf[q, :, y, z]
        student = student.reshape(keep, LANE_BLOCK)
        ebuf[q, core, y, z] = ((student - kept) * (1.0 / math.sqrt(total_kept))).astype(jnp.bfloat16)
        for j in range(1, zs):
            error_level(q, j).start()

    def levels_in(q):
        for j in range(1, zs):
            ref = ebuf.at[q, core, y, lax.rem(z + zs - j, zs)]
            remote(ref, ref, zss.at[q, j - 1], zrs.at[q, j - 1], sibling).wait_recv()
        error_across(q, y).start()

    def across_in(q):
        error_across(q, 1 - y).wait_recv()
        error_sibling(q, core).start()

    def finish(q):
        error_sibling(q, other).wait_recv()
        total = None
        for g in range(2):
            errors = ebuf[q, :, :, :, g * part:(g + 1) * part].reshape(rows_core, LANE_BLOCK)
            term = jnp.dot(turned[g], errors, preferred_element_type=jnp.float32)
            total = term if total is None else total + term
        grad[:, q * LANE_BLOCK:(q + 1) * LANE_BLOCK] = total
        grad_copy(q).start()

    def grad_copy(q):
        columns = pl.ds(q * LANE_BLOCK, LANE_BLOCK)
        return pltpu.make_async_copy(grad.at[:, columns], grad_hbm.at[:, columns], stores.at[q])

    stages = ((product, 0), (error_of, 1), (cores_add, 0), (levels_in, 2), (across_in, 3))
    for wave in range(blocks + 3):
        for stage, lag in stages:
            if 0 <= wave - lag < blocks:
                stage(wave - lag)
        if wave == blocks:
            for q in range(blocks - 3):
                finish(q)
        if wave > blocks:
            finish(wave - 4)
    for q in range(blocks - 1, blocks):
        finish(q)

    for copy in (stats, kept_out, halves):
        copy.wait_send()
    next_out.wait()
    for q in range(blocks):
        for i in range(zs - 1):
            @pl.when((z > 0) & (z + i < zs))
            def _():
                line_copy(0, q, i, z, sibling).wait_send()

            @pl.when((z < zs - 1) & (z - i >= 0))
            def _():
                line_copy(1, q, i, z, sibling).wait_send()
        grad_copy(q).wait()
        h1_copy(q).wait_send()
        h2_copy(q).wait_send()
        sibling_copy(q).wait_send()
        across_copy(q).wait_send()
        for j in range(1, zs):
            error_level(q, j).wait_send()
        error_across(q, y).wait_send()
        error_sibling(q, core).wait_send()
        for e in range(zs):
            for way in range(2):
                @pl.when(e < z if way == 0 else e > z)
                def _():
                    chain_copy(way, q, e, sibling).wait_send()
    for j in range(1, n):
        swap_copy(j).wait_send()
    for j in range(1, 4):
        feature_copy(0, j).wait_send()
    for j in range(4):
        feature_copy(1, j).wait_send()


def fused_shards(images, keep_index, teacher_weight, student_weight):
    n = lax.axis_size("fsdp")
    patches, width = images.shape[1:]
    keep = keep_index.shape[1]
    depth, columns = teacher_weight.shape
    zs, blocks, part = n // 4, columns // LANE_BLOCK, keep // 2
    bf, fl = jnp.bfloat16, jnp.float32
    dma = pltpu.SemaphoreType.DMA
    vm = pltpu.VMEM
    scratch = [
        vm((keep, patches), bf),
        vm((patches, width), bf), vm((depth, columns), fl), vm((depth, columns), fl),
        vm((depth, columns), fl), vm((depth, columns), fl),
        vm((patches, 128), fl), vm((patches, 128), fl),
        vm((2, 2, zs // 2, patches, depth), bf),
        vm((2, 2, zs, patches, depth), bf),
        vm((blocks, zs, depth, LANE_BLOCK), bf),
        vm((blocks, depth, LANE_BLOCK), bf),
        vm((blocks, 2, patches, LANE_BLOCK), fl),
        vm((blocks, 2, patches, LANE_BLOCK), fl),
        vm((blocks, 2, patches, LANE_BLOCK), fl),
        vm((blocks, patches, LANE_BLOCK), bf),
        vm((blocks, patches, LANE_BLOCK), bf),
        vm((n, part, depth), bf),
        vm((n // 2, part, depth), bf),
        vm((2, 2, 2, zs, part, depth), bf),
        vm((2, depth, n * part), bf),
        vm((blocks, 2, 2, zs, part, LANE_BLOCK), fl),
        vm((blocks, 2, 2, zs, part, LANE_BLOCK), bf),
        vm((blocks, 2, 2, zs, part, LANE_BLOCK), bf),
        vm((blocks, 2, zs, part, LANE_BLOCK), bf),
        vm((blocks, 2, zs, part, LANE_BLOCK), bf),
        vm((2, blocks, zs, 2, part, LANE_BLOCK), bf),
        vm((2, blocks, zs, 2, part, LANE_BLOCK), bf),
        vm((blocks, 2, 2, zs, keep, LANE_BLOCK), bf),
        dma((1,)), dma((1,)),
        dma((2, 4)), dma((2, 4)),
        dma((2, blocks, zs - 1)), dma((2, blocks, zs - 1)),
        dma((1,)), dma((1,)),
        dma((n - 1,)), dma((n - 1,)),
        dma((1,)), dma((1,)),
        dma((blocks,)), dma((blocks,)), dma((blocks,)), dma((blocks,)),
        dma((2, blocks, zs)), dma((2, blocks, zs)),
        dma((blocks,)), dma((blocks,)), dma((blocks,)), dma((blocks,)),
        dma((blocks, zs - 1)), dma((blocks, zs - 1)),
        dma((blocks,)), dma((blocks,)), dma((blocks,)), dma((blocks,)),
        dma((3,)), dma((blocks + 1,)),
    ]
    out = jax.ShapeDtypeStruct((depth, columns), fl)
    return pl.pallas_call(
        functools.partial(fused, n, keep * n),
        out_shape=(out, out),
        in_specs=[pl.BlockSpec(memory_space=pltpu.VMEM)] + [pl.BlockSpec(memory_space=pl.ANY)] * 3,
        out_specs=(pl.BlockSpec(memory_space=pl.ANY),) * 2,
        scratch_shapes=scratch,
        compiler_params=pltpu.CompilerParams(
            collective_id=0, has_side_effects=True, vmem_limit_bytes=60 * 2**20),
        cost_estimate=pl.CostEstimate(
            flops=2 * n * depth * columns * (patches + 2 * keep), bytes_accessed=2**24, transcendentals=0),
    )(keep_index, images[0], teacher_weight, student_weight)


def solution(mesh):
    placed = (P("fsdp", None, "tp"), P("fsdp", None), P("fsdp", "tp"), P("fsdp", "tp"))
    fits = mesh.shape["tp"] == 2 and mesh.shape["fsdp"] == 16
    return jax.shard_map(
        fused_shards if fits else shards,
        mesh=mesh,
        in_specs=placed,
        out_specs=(P("fsdp", "tp"), P("fsdp", "tp")),
        check_vma=False,
    )
```

```python
import functools
import math

import jax
import jax.numpy as jnp
from jax import lax
from jax.experimental import pallas as pl
from jax.experimental.pallas import tpu as pltpu
from jax.sharding import PartitionSpec as P

D = 6144


def layer_norm(values):
    floats = values.astype(jnp.float32)
    centre = jnp.mean(floats, axis=-1, keepdims=True)
    centred = floats - centre
    spread = jnp.mean(centred * centred, axis=-1, keepdims=True)
    return (centred * lax.rsqrt(spread + 1e-06)).astype(jnp.bfloat16)


def pick_rows(table, index):
    return jax.vmap(lambda block, rows: block[rows])(table, index)


def row_product(features, piece):
    return jnp.dot(features, piece, preferred_element_type=jnp.float32)


def whole_features(images):
    if lax.axis_size("tp") != 2:
        return lax.all_gather(images, "tp", axis=2, tiled=True)
    other = lax.ppermute(images, "tp", [(0, 1), (1, 0)])
    first = lax.axis_index("tp") == 0
    return jnp.concatenate(
        [jnp.where(first, images, other), jnp.where(first, other, images)], axis=2
    )


def shards(images, keep_index, teacher_weight, student_weight):
    img_count = images.shape[0]
    patch_count = images.shape[1]
    keep_count = keep_index.shape[1]
    columns_dev = teacher_weight.shape[1]
    teacher_next = 0.999 * teacher_weight + (1.0 - 0.999) * student_weight
    teacher_panel = teacher_next.astype(jnp.bfloat16)
    student_panel = student_weight.astype(jnp.bfloat16)
    whole_panel = lax.all_gather(teacher_panel, "fsdp", axis=0, tiled=True)
    normed = layer_norm(whole_features(images))
    flat_all = normed.reshape(img_count * patch_count, D)
    picked = pick_rows(normed, keep_index).reshape(img_count * keep_count, D)
    owned = lax.all_to_all(picked, "fsdp", split_axis=1, concat_axis=0, tiled=True)
    partial = row_product(owned, student_panel).astype(jnp.bfloat16)
    student_out = lax.psum_scatter(partial, "fsdp", scatter_dimension=0, tiled=True)
    student_out = student_out.astype(jnp.float32)
    teacher_out = row_product(flat_all, whole_panel)
    teacher_out = teacher_out.reshape(img_count, patch_count, columns_dev)
    centre = jnp.mean(teacher_out, axis=1, keepdims=True)
    centred_out = teacher_out - centre
    spread = jnp.mean(centred_out * centred_out, axis=1, keepdims=True)
    target = centred_out * lax.rsqrt(spread + 1e-05)
    target_kept = pick_rows(target, keep_index).reshape(img_count * keep_count, columns_dev)
    total_kept = img_count * keep_count * lax.axis_size("fsdp")
    error = ((student_out - target_kept) * (1.0 / math.sqrt(total_kept))).astype(jnp.bfloat16)
    student_grad = lax.dot_general(
        owned,
        lax.all_gather(error, "fsdp", axis=0, tiled=True),
        (((0,), (0,)), ((), ())),
        preferred_element_type=jnp.float32,
    )
    return (teacher_next, student_grad)


MESH = pl.DeviceIdType.MESH
LANE_BLOCK = 256


def fused(n, total_kept, index, images_hbm, tw_hbm, sw_hbm, tnext_hbm, grad_hbm, pick, images, tw, sw, tnext, grad, stat, stat_in, nbuf, xk, wt, ws,
          pt, os_, or_, ys_, yr_, pb, pxs, owned, turned, pf, h1s, h1r, h2s, h2r, h3s, h3r, ebuf,
          sts, str_, xs, xr, ls, lr, ps, pr, as_, ar, ss, sr, h1ss, h1rs, h2ss, h2rs, h3ss, h3rs,
          oss, ors, yss, yrs, zss, zrs, ess, ers, bss, brs, loads, stores):
    f = lax.axis_index("fsdp")
    t = lax.axis_index("tp")
    zs = n // 4
    side = n // 2
    z = lax.div(f, 4)
    spot = lax.rem(f, 4)
    y = lax.div(spot, 2)
    core = lax.rem(spot, 2)
    other = 1 - core
    patches, width = images.shape
    depth = tw.shape[0]
    blocks = tw.shape[1] // LANE_BLOCK
    keep = index.shape[1]
    part = keep // 2
    sibling = (4 * z + 2 * y + other, t)
    across = (4 * z + 2 * (1 - y) + core, t)
    mirror = (f, 1 - t)

    def remote(src, dst, send, recv, device):
        return pltpu.make_async_remote_copy(
            src_ref=src, dst_ref=dst, send_sem=send, recv_sem=recv,
            device_id=device, device_id_type=MESH)

    fetched = [pltpu.make_async_copy(a, b, loads.at[i])
               for i, (a, b) in enumerate(((tw_hbm, tw), (sw_hbm, sw), (images_hbm, images)))]
    for copy in fetched:
        copy.start()

    barrier = pltpu.get_barrier_semaphore()
    for j in range(1, n):
        pl.semaphore_signal(barrier, inc=1, device_id=(lax.rem(f + j, n), t), device_id_type=MESH)
    for j in range(4):
        pl.semaphore_signal(
            barrier, inc=1, device_id=(4 * z + lax.rem(spot + j, 4), 1 - t), device_id_type=MESH)
    chosen = lax.broadcasted_iota(jnp.int32, (patches, keep), 0) == index[...]
    pick[...] = jnp.where(chosen, 1.0, 0.0).T.astype(jnp.bfloat16)
    pl.semaphore_wait(barrier, n + 3)

    def line_copy(way, q, i, source, to):
        ref = wt.at[q, source]
        return remote(ref, ref, ls.at[way, q, i], lr.at[way, q, i], to)

    down = (f - 4, t)
    up = (f + 4, t)
    tile = 64
    fetched[0].wait()
    fetched[1].wait()
    for q in range(blocks):
        columns = slice(q * LANE_BLOCK, (q + 1) * LANE_BLOCK)

        @pl.loop(0, depth // tile)
        def _(i):
            rows = pl.ds(pl.multiple_of(i * tile, tile), tile)
            student = sw[rows, columns]
            following = 0.999 * tw[rows, columns] + (1.0 - 0.999) * student
            tnext[rows, columns] = following
            wt[q, z, rows, :] = following.astype(jnp.bfloat16)
            ws[q, rows, :] = student.astype(jnp.bfloat16)

        @pl.when(z > 0)
        def _():
            line_copy(0, q, 0, z, down).start()

        @pl.when(z < zs - 1)
        def _():
            line_copy(1, q, 0, z, up).start()

    next_out = pltpu.make_async_copy(tnext, tnext_hbm, stores.at[blocks])
    next_out.start()

    fetched[2].wait()
    lane = lax.broadcasted_iota(jnp.int32, (16, 128), 1)

    @pl.loop(0, patches // 16)
    def _(i):
        rows = pl.ds(pl.multiple_of(i * 16, 16), 16)
        values = images[rows, :].astype(jnp.float32)
        centre = jnp.sum(values, axis=1, keepdims=True) * (1.0 / width)
        values = values - centre
        spread = jnp.sum(values * values, axis=1, keepdims=True)
        stat[rows, :] = jnp.where(lane < 64, centre, spread)

    stats = remote(stat, stat_in, sts.at[0], str_.at[0], mirror)
    stats.start()

    def pump(i, q):
        @pl.when(z + 1 + i < zs)
        def _():
            line_copy(0, q, i, z + 1 + i, sibling).wait_recv()
            if i < zs - 2:
                @pl.when(z > 0)
                def _():
                    line_copy(0, q, i + 1, z + 1 + i, down).start()

        @pl.when(z - 1 - i >= 0)
        def _():
            line_copy(1, q, i, z - 1 - i, sibling).wait_recv()
            if i < zs - 2:
                @pl.when(z < zs - 1)
                def _():
                    line_copy(1, q, i + 1, z - 1 - i, up).start()

    stats.wait_recv()

    @pl.loop(0, patches // 16)
    def _(i):
        rows = pl.ds(pl.multiple_of(i * 16, 16), 16)
        here, there = stat[rows, :], stat_in[rows, :]
        centre = (here[:, 0:1] + there[:, 0:1]) * 0.5
        apart = here[:, 0:1] - there[:, 0:1]
        spread = (here[:, 64:65] + there[:, 64:65]) * (0.5 / width) + apart * apart * 0.25
        scaled = ((images[rows, :].astype(jnp.float32) - centre) * lax.rsqrt(spread + 1e-06)).astype(jnp.bfloat16)
        for j in range(side):
            nbuf[j % 4 // 2, j % 2, j // 4, rows, :] = scaled[:, j * depth:(j + 1) * depth]

    @pl.loop(0, side // 4)
    def _(level):
        for j in range(4):
            rows = jnp.dot(pick[...], nbuf[j // 2, j % 2, level],
                           preferred_element_type=jnp.float32).astype(jnp.bfloat16)
            pb[side * t + 4 * level + j] = rows[:part]
            pxs[4 * level + j] = rows[part:]

    kept_out = remote(pxs, pb.at[pl.ds(side * t, side)], ps.at[0], pr.at[0], mirror)
    kept_out.start()

    def feature_copy(plane, j):
        to = lax.rem(spot + j, 4)
        return remote(nbuf.at[lax.div(to, 2), lax.rem(to, 2)], xk.at[y, core, pl.ds(2 * t, 2)],
                      xs.at[plane, j], xr.at[plane, j],
                      (4 * z + to, t if plane == 0 else 1 - t))

    xk[y, core, pl.ds(2 * t, 2)] = nbuf[y, core]
    kept_in = remote(pxs, pb.at[pl.ds(side * (1 - t), side)], ps.at[0], pr.at[0], mirror)
    kept_in.wait_recv()

    def half_of(device):
        return lax.rem(t + lax.div(device, side), 2)

    def swap_copy(j):
        to = lax.rem(f + j, n)
        return remote(pb.at[to], owned.at[half_of(to), core, y, z], as_.at[j - 1], ar.at[j - 1], (to, t))

    mine = half_of(f)
    for j in range(1, n):
        swap_copy(j).start()
    owned[mine, core, y, z] = pb[f]
    for j in range(1, 4):
        feature_copy(0, j).start()
    for j in range(2):
        feature_copy(1, j).start()

    for q in range(blocks // 2):
        pump(0, q)

    for j in range(1, n):
        origin = lax.rem(f + n - j, n)
        remote(pb.at[0],
               owned.at[mine, lax.rem(origin, 2), lax.div(lax.rem(origin, 4), 2), lax.div(origin, 4)],
               as_.at[j - 1], ar.at[j - 1], (origin, t)).wait_recv()
    halves = remote(owned.at[mine], owned.at[mine], ss.at[0], sr.at[0], mirror)
    halves.start()
    for j in range(2, 4):
        feature_copy(1, j).start()
    for q in range(blocks // 2, blocks):
        pump(0, q)
    remote(owned.at[1 - mine], owned.at[1 - mine], ss.at[0], sr.at[0], mirror).wait_recv()

    split = (2, 2, zs, part, LANE_BLOCK)
    rows_core = 4 * zs * part

    def h1_copy(q):
        return remote(h1s.at[q], h1r.at[q], h1ss.at[q], h1rs.at[q], sibling)

    def h2_copy(q):
        return remote(h2s.at[q], h2r.at[q], h2ss.at[q], h2rs.at[q], across)

    def chain_copy(way, q, e, to):
        return remote(h3s.at[way, q, e], h3r.at[way, q, e], h3ss.at[way, q, e], h3rs.at[way, q, e], to)

    def chain(q, way, first):
        for e in range(zs):
            ahead = e < z if way == 0 else e > z

            @pl.when(ahead)
            def _():
                value = pf[q, :, y, e]
                if not first:
                    chain_copy(way, q, e, sibling).wait_recv()
                    value = value + h3r[way, q, e].astype(jnp.float32)
                h3s[way, q, e] = value.astype(jnp.bfloat16)
                chain_copy(way, q, e, down if way == 0 else up).start()

    def chain_step(q, hop):
        if hop == 0:
            @pl.when(z == zs - 1)
            def _():
                chain(q, 0, True)

            @pl.when(z == 0)
            def _():
                chain(q, 1, True)
        else:
            @pl.when(z == zs - 1 - hop)
            def _():
                chain(q, 0, False)

            @pl.when(z == hop)
            def _():
                chain(q, 1, False)

    @pl.loop(0, blocks)
    def _(q):
        panel = ws[q]
        send = jnp.dot(owned[:, other].reshape(rows_core, depth), panel,
                       preferred_element_type=jnp.float32)
        h1s[q] = send.astype(jnp.bfloat16).reshape(split)
        h1_copy(q).start()
        own = jnp.dot(owned[:, core].reshape(rows_core, depth), panel,
                      preferred_element_type=jnp.float32)
        pf[q] = own.reshape(split)

    for q in range(blocks // 2):
        pump(1, q)

    @pl.loop(0, blocks)
    def _(q):
        h1_copy(q).wait_recv()
        for g in range(2):
            h2s[q, g] = (pf[q, g, 1 - y] + h1r[q, g, 1 - y].astype(jnp.float32)).astype(jnp.bfloat16)
            pf[q, g, y] += h1r[q, g, y].astype(jnp.float32)
        h2_copy(q).start()

    for g in range(2):
        turned[g] = owned[g].reshape(rows_core, depth).T

    def student(q):
        h2_copy(q).wait_recv()

        @pl.loop(0, zs)
        def _(level):
            for g in range(2):
                pf[q, g, y, level] += h2r[q, g, level].astype(jnp.float32)

        chain_step(q, 0)

    def hops(q):
        for hop in range(1, zs - 1):
            if 0 <= q - hop < blocks:
                chain_step(q - hop, hop)

    ahead = blocks // 2
    for q in range(ahead):
        if ahead + q < blocks:
            pump(1, ahead + q)
        student(q)
        hops(q)

    def feature_wait(plane, j):
        origin = lax.rem(spot + 4 - j, 4)
        first = 2 * t if plane == 0 else 2 * (1 - t)
        remote(nbuf.at[0, 0], xk.at[lax.div(origin, 2), lax.rem(origin, 2), pl.ds(first, 2)],
               xs.at[plane, j], xr.at[plane, j], sibling).wait_recv()

    for j in range(1, 4):
        feature_wait(0, j)
    for j in range(4):
        feature_wait(1, j)

    def sibling_copy(q):
        return remote(os_.at[q], or_.at[q], oss.at[q], ors.at[q], sibling)

    def across_copy(q):
        return remote(ys_.at[q], yr_.at[q], yss.at[q], yrs.at[q], across)

    def error_level(q, j):
        ref = ebuf.at[q, core, y, z]
        return remote(ref, ref, zss.at[q, j - 1], zrs.at[q, j - 1], (4 * lax.rem(z + j, zs) + spot, t))

    def error_across(q, row):
        ref = ebuf.at[q, core, row]
        return remote(ref, ref, ess.at[q], ers.at[q], across)

    def error_sibling(q, owner):
        ref = ebuf.at[q, owner]
        return remote(ref, ref, bss.at[q], brs.at[q], sibling)

    def product(q):
        if zs > 2:
            pump(zs - 2, q)

        @pl.loop(0, 2)
        def _(row):
            for target, owner in ((os_, other), (pt, core)):
                total = jnp.dot(xk[row, owner, 0], wt[q, 0], preferred_element_type=jnp.float32)
                for level in range(1, zs):
                    total += jnp.dot(xk[row, owner, level], wt[q, level],
                                     preferred_element_type=jnp.float32)
                target[q, row] = total

        sibling_copy(q).start()

    def cores_add(q):
        sibling_copy(q).wait_recv()
        ys_[q] = (pt[q, 1 - y] + or_[q, 1 - y]).astype(jnp.bfloat16)
        across_copy(q).start()
        pt[q, y] += or_[q, y]

    def error_of(q):
        for way in range(2):
            @pl.when(z < zs - 1 if way == 0 else z > 0)
            def _():
                chain_copy(way, q, z, sibling).wait_recv()
                pf[q, :, y, z] += h3r[way, q, z].astype(jnp.float32)
        across_copy(q).wait_recv()
        value = pt[q, y] + yr_[q].astype(jnp.float32)
        centre = jnp.sum(value, axis=0, keepdims=True) * (1.0 / patches)
        value = value - centre
        spread = jnp.sum(value * value, axis=0, keepdims=True) * (1.0 / patches)
        target = value * lax.rsqrt(spread + 1e-05)
        upper = target.astype(jnp.bfloat16)
        lower = (target - upper.astype(jnp.float32)).astype(jnp.bfloat16)
        kept = (jnp.dot(pick[...], upper, preferred_element_type=jnp.float32)
                + jnp.dot(pick[...], lower, preferred_element_type=jnp.float32))
        student = pf[q, :, y, z]
        student = student.reshape(keep, LANE_BLOCK)
        ebuf[q, core, y, z] = ((student - kept) * (1.0 / math.sqrt(total_kept))).astype(jnp.bfloat16)
        for j in range(1, zs):
            error_level(q, j).start()

    def levels_in(q):
        for j in range(1, zs):
            ref = ebuf.at[q, core, y, lax.rem(z + zs - j, zs)]
            remote(ref, ref, zss.at[q, j - 1], zrs.at[q, j - 1], sibling).wait_recv()
        error_across(q, y).start()

    def across_in(q):
        error_across(q, 1 - y).wait_recv()
        error_sibling(q, core).start()

    def finish(q):
        error_sibling(q, other).wait_recv()
        total = None
        for g in range(2):
            errors = ebuf[q, :, :, :, g * part:(g + 1) * part].reshape(rows_core, LANE_BLOCK)
            term = jnp.dot(turned[g], errors, preferred_element_type=jnp.float32)
            total = term if total is None else total + term
        grad[:, q * LANE_BLOCK:(q + 1) * LANE_BLOCK] = total
        grad_copy(q).start()

    def grad_copy(q):
        columns = pl.ds(q * LANE_BLOCK, LANE_BLOCK)
        return pltpu.make_async_copy(grad.at[:, columns], grad_hbm.at[:, columns], stores.at[q])

    stages = ((product, 0), (error_of, 1), (cores_add, 0), (levels_in, 2), (across_in, 3))
    for wave in range(blocks + 3):
        for stage, lag in stages:
            if 0 <= wave - lag < blocks:
                stage(wave - lag)
            if stage is product:
                if wave + ahead < blocks:
                    student(wave + ahead)
                hops(wave + ahead)
        if wave == blocks:
            for q in range(blocks - 3):
                finish(q)
        if wave > blocks:
            finish(wave - 4)
    for q in range(blocks - 1, blocks):
        finish(q)

    for copy in (stats, kept_out, halves):
        copy.wait_send()
    next_out.wait()
    for q in range(blocks):
        for i in range(zs - 1):
            @pl.when((z > 0) & (z + i < zs))
            def _():
                line_copy(0, q, i, z, sibling).wait_send()

            @pl.when((z < zs - 1) & (z - i >= 0))
            def _():
                line_copy(1, q, i, z, sibling).wait_send()
        grad_copy(q).wait()
        h1_copy(q).wait_send()
        h2_copy(q).wait_send()
        sibling_copy(q).wait_send()
        across_copy(q).wait_send()
        for j in range(1, zs):
            error_level(q, j).wait_send()
        error_across(q, y).wait_send()
        error_sibling(q, core).wait_send()
        for e in range(zs):
            for way in range(2):
                @pl.when(e < z if way == 0 else e > z)
                def _():
                    chain_copy(way, q, e, sibling).wait_send()
    for j in range(1, n):
        swap_copy(j).wait_send()
    for j in range(1, 4):
        feature_copy(0, j).wait_send()
    for j in range(4):
        feature_copy(1, j).wait_send()


def fused_shards(images, keep_index, teacher_weight, student_weight):
    n = lax.axis_size("fsdp")
    patches, width = images.shape[1:]
    keep = keep_index.shape[1]
    depth, columns = teacher_weight.shape
    zs, blocks, part = n // 4, columns // LANE_BLOCK, keep // 2
    bf, fl = jnp.bfloat16, jnp.float32
    dma = pltpu.SemaphoreType.DMA
    vm = pltpu.VMEM
    scratch = [
        vm((keep, patches), bf),
        vm((patches, width), bf), vm((depth, columns), fl), vm((depth, columns), fl),
        vm((depth, columns), fl), vm((depth, columns), fl),
        vm((patches, 128), fl), vm((patches, 128), fl),
        vm((2, 2, zs // 2, patches, depth), bf),
        vm((2, 2, zs, patches, depth), bf),
        vm((blocks, zs, depth, LANE_BLOCK), bf),
        vm((blocks, depth, LANE_BLOCK), bf),
        vm((blocks, 2, patches, LANE_BLOCK), fl),
        vm((blocks, 2, patches, LANE_BLOCK), fl),
        vm((blocks, 2, patches, LANE_BLOCK), fl),
        vm((blocks, patches, LANE_BLOCK), bf),
        vm((blocks, patches, LANE_BLOCK), bf),
        vm((n, part, depth), bf),
        vm((n // 2, part, depth), bf),
        vm((2, 2, 2, zs, part, depth), bf),
        vm((2, depth, n * part), bf),
        vm((blocks, 2, 2, zs, part, LANE_BLOCK), fl),
        vm((blocks, 2, 2, zs, part, LANE_BLOCK), bf),
        vm((blocks, 2, 2, zs, part, LANE_BLOCK), bf),
        vm((blocks, 2, zs, part, LANE_BLOCK), bf),
        vm((blocks, 2, zs, part, LANE_BLOCK), bf),
        vm((2, blocks, zs, 2, part, LANE_BLOCK), bf),
        vm((2, blocks, zs, 2, part, LANE_BLOCK), bf),
        vm((blocks, 2, 2, zs, keep, LANE_BLOCK), bf),
        dma((1,)), dma((1,)),
        dma((2, 4)), dma((2, 4)),
        dma((2, blocks, zs - 1)), dma((2, blocks, zs - 1)),
        dma((1,)), dma((1,)),
        dma((n - 1,)), dma((n - 1,)),
        dma((1,)), dma((1,)),
        dma((blocks,)), dma((blocks,)), dma((blocks,)), dma((blocks,)),
        dma((2, blocks, zs)), dma((2, blocks, zs)),
        dma((blocks,)), dma((blocks,)), dma((blocks,)), dma((blocks,)),
        dma((blocks, zs - 1)), dma((blocks, zs - 1)),
        dma((blocks,)), dma((blocks,)), dma((blocks,)), dma((blocks,)),
        dma((3,)), dma((blocks + 1,)),
    ]
    out = jax.ShapeDtypeStruct((depth, columns), fl)
    return pl.pallas_call(
        functools.partial(fused, n, keep * n),
        out_shape=(out, out),
        in_specs=[pl.BlockSpec(memory_space=pltpu.VMEM)] + [pl.BlockSpec(memory_space=pl.ANY)] * 3,
        out_specs=(pl.BlockSpec(memory_space=pl.ANY),) * 2,
        scratch_shapes=scratch,
        compiler_params=pltpu.CompilerParams(
            collective_id=0, has_side_effects=True, vmem_limit_bytes=60 * 2**20),
        cost_estimate=pl.CostEstimate(
            flops=2 * n * depth * columns * (patches + 2 * keep), bytes_accessed=2**24, transcendentals=0),
    )(keep_index, images[0], teacher_weight, student_weight)


def solution(mesh):
    placed = (P("fsdp", None, "tp"), P("fsdp", None), P("fsdp", "tp"), P("fsdp", "tp"))
    fits = mesh.shape["tp"] == 2 and mesh.shape["fsdp"] == 16
    return jax.shard_map(
        fused_shards if fits else shards,
        mesh=mesh,
        in_specs=placed,
        out_specs=(P("fsdp", "tp"), P("fsdp", "tp")),
        check_vma=False,
    )
```
